32 devices in a mesh: sub: 8 (over z, x), crs: 4 (over y, core).
Axes of the slice: x: 2, y: 2, z: 4, core: 2. Of those that a mesh axis runs over, the one named last changes fastest.
Arguments:
- residual: float32 [32, 6, 3072], P('sub', None, 'crs'), may hold values from -6 to 6
- stiffness: float32 [32, 6, 3072], P('sub', None, 'crs'), may hold values from 0.1 to 10
- solid: int32 [32, 6, 16], P('sub', None, 'crs'), may hold values 0 or 1
- inverses: bfloat16 [32, 6, 192, 3072], P('sub', None, None, 'crs')
- coarse_basis: bfloat16 [32, 24, 6, 3072], P('sub', None, None, 'crs'), may hold values from -0.29882812 to 0.29882812
- assign: int32 [32], replicated, may hold values from 0 to 31, as said below
- corners: int32 [32, 8], P('sub'), may hold values from 0 to 31, as said below
- coarse_inverse: float32 [96, 96], P('crs')
Outputs:
- preconditioned: float32 [32, 6, 3072], P('sub', None, 'crs')
- inner_value: float32 [1], replicated
The draws below stay inside these ranges and needn't reach their ends.
Inputs may be any that keep to these rules, and one draw needn't show every extreme that they name: assign is a permutation of the 32 subdomain numbers, set at run time by the load balancer, so a subdomain's neighbours may be held on any devices. corners[t, c] is the number of corner c = 4 cx + 2 cy + cz of subdomain assign[t], the grid vertex at its place plus (cx, cy, cz) taken periodically, under one fixed permutation of the 32 vertices.
All inputs are finite; a program needn't handle non-finite values. No bound on the sum of `solid` on one device may be relied on, other than what follows from the above.
Results may differ from the reference program's by a relative error of at most 0.0028.
Values sent between devices are 32-bit elements; how exact they have to be, the bound alone decides.
A program may use at most 128 MiB of HBM per device.

```python
import math
import jax
import jax.numpy as jnp
from jax import lax

PATCHES = 16
K = 192
NPRIM = 24
SUBS = 32
NC = 96


def layout_tables(key):
    order = jax.random.permutation(jax.random.fold_in(key, 11), SUBS).astype(jnp.int32)
    relabel = jax.random.permutation(jax.random.fold_in(key, 12), SUBS).astype(jnp.int32)
    return (order, relabel)


def draw_assign(key, part):
    return layout_tables(key)[0]


def draw_corners(key, part):
    order, relabel = layout_tables(key)
    depth = SUBS // 16
    coord_a = order // (4 * depth)
    coord_b = order // depth % 4
    coord_c = order % depth
    listed = []
    for corner in range(8):
        step_a = corner // 4
        step_b = corner // 2 % 2
        step_c = corner % 2
        vertex = ((coord_a + step_a) % 4 * 4 + (coord_b + step_b) % 4) * depth + (coord_c + step_c) % depth
        listed.append(relabel[vertex])
    return jnp.stack(listed, axis=1).astype(jnp.int32)


def draw_inverses(key, part):
    diag_key = jax.random.fold_in(key, 21)
    off_key = jax.random.fold_in(key, 22)
    diagonal = jnp.exp(jax.random.uniform(diag_key, (SUBS, 6, PATCHES, K), jnp.float32, 0.0, 0.7))
    spread = jax.random.normal(off_key, (SUBS, 6, PATCHES, K, K), jnp.float32) * (0.4 / K ** 0.5)
    identity = jnp.eye(K, dtype=jnp.float32)
    blocks = spread + identity * diagonal[..., None]
    return blocks.transpose(0, 1, 3, 2, 4).reshape(SUBS, 6, K, PATCHES * K).astype(jnp.bfloat16)


def draw_coarse_inverse(key, part):
    diag_key = jax.random.fold_in(key, 31)
    off_key = jax.random.fold_in(key, 32)
    diagonal = jnp.exp(jax.random.uniform(diag_key, (NC,), jnp.float32, -3.5, -2.3))
    spread = jax.random.normal(off_key, (NC, NC), jnp.float32) * (0.05 / NC ** 0.5)
    identity = jnp.eye(NC, dtype=jnp.float32)
    return spread + identity * diagonal[None, :]


def touch_ends(result, rng, low, top_value):
    longest = result.shape.index(max(result.shape))
    spots = []
    for shift in (0, 1):
        where = [jax.random.randint(jax.random.fold_in(rng, axis), (), 0, length) for axis, length in enumerate(result.shape)]
        where[longest] = (where[longest] + shift) % result.shape[longest]
        spots.append(tuple(where))
    return result.at[spots[0]].set(low).at[spots[1]].set(top_value)


def level_of(stream_key, extent, pieces, low, largest):
    gain = 1.0
    for axis_at, blocks in pieces:
        steps = jax.random.uniform(jax.random.fold_in(jax.random.fold_in(stream_key, 6), axis_at), (blocks,), jnp.float32, low / len(pieces), largest / len(pieces))
        gain = gain * jnp.repeat(jnp.exp(steps), extent[axis_at] // blocks).reshape((-1,) + (1,) * (len(extent) - 1 - axis_at))
    return gain


def noise(own_key, shape, scale, bound, pieces=(), held_as=jnp.bfloat16):
    entries = scale * jax.random.normal(own_key, shape, jnp.float32)
    if pieces:
        entries = entries * level_of(own_key, shape, pieces, -0.22, 0.18)
    return jnp.clip(entries, -bound, bound).astype(held_as)


def setup_inputs(seed: int = 0) -> dict:
    splits = jax.random.split(jax.random.key(seed), 9)
    residual = noise(splits[0], (SUBS, 6, PATCHES * K), 1.0, 6.0, ((0, 8), (2, 4)), jnp.float32)
    stiffness = jnp.clip(jnp.exp(math.log(10.0) - 4.6051702 * jax.random.uniform(splits[1], (SUBS, 6, PATCHES * K), jnp.float32) ** level_of(splits[1], (SUBS, 6, PATCHES * K), ((0, 8), (2, 4)), -0.2, 0.2)), 0.1, 10.0)
    solid = touch_ends((jax.random.randint(splits[2], (SUBS, 6, PATCHES), 0, 4) < 3).astype(jnp.int32), jax.random.fold_in(splits[2], 1), 0, 1)
    inverses = draw_inverses(jax.random.fold_in(splits[8], 71), 0)
    coarse_basis = noise(splits[4], (SUBS, NPRIM, 6, PATCHES * K), 0.05, 0.29882812, ((0, 8), (3, 4)))
    assign = draw_assign(jax.random.fold_in(splits[8], 71), 0)
    corners = draw_corners(jax.random.fold_in(splits[8], 71), 0)
    coarse_inverse = draw_coarse_inverse(jax.random.fold_in(splits[8], 71), 0)
    return dict(residual=residual, stiffness=stiffness, solid=solid, inverses=inverses, coarse_basis=coarse_basis, assign=assign, corners=corners, coarse_inverse=coarse_inverse)


def partner_rows(assign, subs):
    depth = subs // 16
    slots = jnp.arange(subs, dtype=jnp.int32)
    inverse = jnp.sum(slots[:, None] * (assign[:, None] == slots[None, :]).astype(jnp.int32), axis=0)
    coord_a = assign // (4 * depth)
    coord_b = (assign // depth) % 4
    coord_c = assign % depth

    def number(first, second, third):
        return (first * 4 + second) * depth + third

    neighbours = jnp.stack([
        number((coord_a + 1) % 4, coord_b, coord_c),
        number(coord_a, (coord_b + 1) % 4, coord_c),
        number(coord_a, coord_b, (coord_c + 1) % depth),
        number((coord_a + 3) % 4, coord_b, coord_c),
        number(coord_a, (coord_b + 3) % 4, coord_c),
        number(coord_a, coord_b, (coord_c + depth - 1) % depth)], axis=1)
    partner_slot = inverse[neighbours]
    partner_face = jnp.array([3, 4, 5, 0, 1, 2], dtype=jnp.int32)
    return (partner_slot * 6 + partner_face[None, :]).reshape(-1).astype(jnp.int32)


def reference(residual, stiffness, solid, inverses, coarse_basis, assign, corners, coarse_inverse):
    subs = residual.shape[0]
    rows = partner_rows(assign, subs)
    flat_r = residual.reshape(subs * 6, -1)
    flat_k = stiffness.reshape(subs * 6, -1)
    partner_r = flat_r[rows]
    partner_k = flat_k[rows]
    weight = flat_k / (flat_k + partner_k)
    weight_partner = partner_k / (flat_k + partner_k)
    solid_f = jnp.repeat(solid.astype(jnp.float32), K, axis=2)
    restricted = (solid_f * (weight * (flat_r + partner_r)).reshape(residual.shape)).astype(jnp.bfloat16)

    def solve_one(pair):
        blocks = pair[0].astype(jnp.float32).reshape(6, K, PATCHES, K)
        vector = pair[1].astype(jnp.float32).reshape(6, PATCHES, K)
        return jnp.einsum('fipj,fpj->fpi', blocks, vector).reshape(6, PATCHES * K)

    local = lax.map(solve_one, (inverses, restricted))
    coarse_part = jnp.einsum('scfk,sfk->sc', coarse_basis.astype(jnp.float32), restricted.astype(jnp.float32))
    index = (3 * corners[:, :, None] + jnp.arange(3, dtype=jnp.int32)[None, None, :]).reshape(subs, 24)
    coarse_residual = jnp.zeros((3 * subs,), jnp.float32).at[index.reshape(-1)].add(coarse_part.reshape(-1))
    coarse_solution = jnp.dot(coarse_residual, coarse_inverse, precision=lax.Precision.HIGHEST)
    corner_values = coarse_solution[index].astype(jnp.bfloat16)
    correction = jnp.einsum('sc,scfk->sfk', corner_values.astype(jnp.float32), coarse_basis.astype(jnp.float32))
    solution = solid_f * (local + correction)
    flat_u = solution.reshape(subs * 6, -1)
    preconditioned = (weight * flat_u + weight_partner * flat_u[rows]).reshape(residual.shape)
    inner_value = jnp.sum(residual * preconditioned).reshape(1)
    return preconditioned, inner_value
```

```python
import functools

import jax
import jax.numpy as jnp
from jax import lax
from jax.experimental import pallas as pl
from jax.experimental.pallas import tpu as pltpu
from jax.sharding import PartitionSpec as P

F32 = jnp.float32
BF16 = jnp.bfloat16
LANES = 128


def iota(shape, dim):
    return lax.broadcasted_iota(jnp.int32, shape, dim)


def split2(x):
    high = x.astype(BF16)
    low = (x - high.astype(F32)).astype(BF16)
    return high, low


def kernel(
    cfg,
    r_ref, k_ref, solid_ref, inv_hbm, basis_hbm, assign_ref, corners_ref, ci_ref,
    out_ref, inner_ref,
    inv, basis, s1, rb1, rx1, wts, tb2, tx2, b2, s3, rb3, rx3, tb4, tx4, b4,
    perm, smf, sm, xf, loc, corr, vt, sel, onehot, cv, ci,
    ca_s, ca_r, cb_s, cb_r, ia_s, ia_r, ib_s, ib_r,
    send, recv, own, load, small_send, small_recv, ci_send, ci_recv,
):
    n, m, slots, tiles, patches, entries, subs = cfg
    depth = subs // 16
    units = 3 * tiles
    base = units // n
    extra_any = units % n != 0
    rows_unit = 2 * slots
    rows_all = n * rows_unit
    rows_here = 6 * slots
    width = tiles * LANES
    nprim = basis.shape[1]
    coarse = ci_ref.shape[1]
    me = lax.axis_index("sub")
    mc = lax.axis_index("crs")

    def first(p):
        return (p * units + n - 1) // n

    def has_extra(p):
        return first(p + 1) - first(p) > base

    def row_of(l, f):
        return (f % 3) * rows_unit + (f // 3) * slots + l

    inv_load = [pltpu.make_async_copy(inv_hbm.at[l], inv.at[l], load.at[l]) for l in range(slots)]
    basis_load = pltpu.make_async_copy(basis_hbm, basis, load.at[slots])
    basis_load.start()
    for c in inv_load:
        c.start()

    def each_sub(body):
        if n <= 8:
            for k in range(1, n):
                body(k, lax.rem(me + k, n))
        else:
            def step(k, carry):
                body(k, lax.rem(me + k, n))
                return carry
            lax.fori_loop(1, n, step, 0)

    barrier = pltpu.get_barrier_semaphore()

    def greet(k, p):
        pl.semaphore_signal(barrier, inc=1, device_id={"sub": p}, device_id_type=pl.DeviceIdType.MESH)

    each_sub(greet)
    for k in range(1, m):
        pl.semaphore_signal(barrier, inc=1, device_id={"crs": lax.rem(mc + k, m)}, device_id_type=pl.DeviceIdType.MESH)

    for a, ref in enumerate((r_ref, k_ref)):
        for l in range(slots):
            for f in range(6):
                for ct in range(tiles):
                    row = (f // 3) * slots + l
                    s1[(f % 3) * tiles + ct, a, row:row + 1, :] = ref[l, f:f + 1, ct * LANES:(ct + 1) * LANES]

    def to_sub(src, dst, stage, kind, k, p):
        return pltpu.make_async_remote_copy(
            src_ref=src, dst_ref=dst, send_sem=send.at[stage, kind, k], recv_sem=recv.at[stage, kind, me],
            device_id={"sub": p}, device_id_type=pl.DeviceIdType.MESH)

    def from_sub(dst, stage, kind, p):
        pltpu.make_async_remote_copy(
            src_ref=dst, dst_ref=dst, send_sem=send.at[stage, kind, 0], recv_sem=recv.at[stage, kind, p],
            device_id={"sub": p}, device_id_type=pl.DeviceIdType.MESH).wait_recv()

    def spread(src, dst_base, dst_extra, stage):
        def go(k, p):
            if base:
                to_sub(src.at[pl.ds(first(p), base)], dst_base.at[me], stage, 0, k, p).start()
            if extra_any:
                @pl.when(has_extra(p))
                def _():
                    to_sub(src.at[first(p) + base], dst_extra.at[me], stage, 1, k, p).start()
        each_sub(go)
        if base:
            pltpu.make_async_copy(src.at[pl.ds(first(me), base)], dst_base.at[me], own.at[stage, 0]).start()
        if extra_any:
            @pl.when(has_extra(me))
            def _():
                pltpu.make_async_copy(src.at[first(me) + base], dst_extra.at[me], own.at[stage, 1]).start()

    def spread_wait(src, dst_base, dst_extra, stage):
        if base:
            pltpu.make_async_copy(src.at[pl.ds(first(me), base)], dst_base.at[me], own.at[stage, 0]).wait()
            each_sub(lambda k, p: from_sub(dst_base.at[p], stage, 0, p))
        if extra_any:
            @pl.when(has_extra(me))
            def _():
                pltpu.make_async_copy(src.at[first(me) + base], dst_extra.at[me], own.at[stage, 1]).wait()
                each_sub(lambda k, p: from_sub(dst_extra.at[p], stage, 1, p))

    def spread_done(src, dst_base, dst_extra, stage):
        def go(k, p):
            if base:
                to_sub(src.at[pl.ds(first(p), base)], dst_base.at[me], stage, 0, k, p).wait_send()
            if extra_any:
                @pl.when(has_extra(p))
                def _():
                    to_sub(src.at[first(p) + base], dst_extra.at[me], stage, 1, k, p).wait_send()
        each_sub(go)

    def back(src_base, src_extra, dst, stage):
        def go(k, p):
            if base:
                to_sub(src_base.at[p], dst.at[pl.ds(first(me), base)], stage, 0, k, p).start()
        each_sub(go)
        if base:
            pltpu.make_async_copy(src_base.at[me], dst.at[pl.ds(first(me), base)], own.at[stage, 0]).start()
        if extra_any:
            @pl.when(has_extra(me))
            def _():
                each_sub(lambda k, p: to_sub(src_extra.at[p], dst.at[first(me) + base], stage, 1, k, p).start())
                pltpu.make_async_copy(src_extra.at[me], dst.at[first(me) + base], own.at[stage, 1]).start()

    def back_wait(src_base, src_extra, dst, stage):
        if base:
            pltpu.make_async_copy(src_base.at[me], dst.at[pl.ds(first(me), base)], own.at[stage, 0]).wait()
        if extra_any:
            @pl.when(has_extra(me))
            def _():
                pltpu.make_async_copy(src_extra.at[me], dst.at[first(me) + base], own.at[stage, 1]).wait()

        def go(k, p):
            if base:
                from_sub(dst.at[pl.ds(first(p), base)], stage, 0, p)
            if extra_any:
                @pl.when(has_extra(p))
                def _():
                    from_sub(dst.at[first(p) + base], stage, 1, p)
        each_sub(go)

    def back_done(src_base, src_extra, dst, stage):
        if base:
            each_sub(lambda k, p: to_sub(src_base.at[p], dst.at[pl.ds(first(me), base)], stage, 0, k, p).wait_send())
        if extra_any:
            @pl.when(has_extra(me))
            def _():
                each_sub(lambda k, p: to_sub(src_extra.at[p], dst.at[first(me) + base], stage, 1, k, p).wait_send())

    def small_sub(src, dst, which, k, p):
        return pltpu.make_async_remote_copy(
            src_ref=src, dst_ref=dst.at[me], send_sem=small_send.at[which, k], recv_sem=small_recv.at[which, me],
            device_id={"sub": p}, device_id_type=pl.DeviceIdType.MESH)

    def small_sub_wait(dst, which, p):
        pltpu.make_async_remote_copy(
            src_ref=dst.at[p], dst_ref=dst.at[p], send_sem=small_send.at[which, 0], recv_sem=small_recv.at[which, p],
            device_id={"sub": p}, device_id_type=pl.DeviceIdType.MESH).wait_recv()

    def small_crs(src, dst, send_sem, recv_sem, k):
        return pltpu.make_async_remote_copy(
            src_ref=src, dst_ref=dst.at[mc], send_sem=send_sem.at[k], recv_sem=recv_sem.at[mc],
            device_id={"crs": lax.rem(mc + k, m)}, device_id_type=pl.DeviceIdType.MESH)

    def small_crs_wait(dst, send_sem, recv_sem, k):
        q = lax.rem(mc + k, m)
        pltpu.make_async_remote_copy(
            src_ref=dst.at[q], dst_ref=dst.at[q], send_sem=send_sem.at[0], recv_sem=recv_sem.at[q],
            device_id={"crs": q}, device_id_type=pl.DeviceIdType.MESH).wait_recv()

    pl.semaphore_wait(barrier, n - 1 + m - 1)
    spread(s1, rb1, rx1, 0)
    for k in range(1, m):
        small_crs(ci_ref, ci, ci_send, ci_recv, k).start()

    ci[mc] = ci_ref[...]
    assign_row = assign_ref[...]
    pick = iota((subs, subs), 0) == iota((subs, subs), 1)
    assign_col = jnp.sum(jnp.where(pick, assign_row, 0), axis=1, keepdims=True)
    slot_col = iota((rows_all, subs), 0) // rows_unit * slots + iota((rows_all, subs), 0) % slots
    a_col = jnp.sum(jnp.where(slot_col == iota((rows_all, subs), 1), assign_row, 0), axis=1, keepdims=True)
    slot_row = iota((subs, rows_all), 1) // rows_unit * slots + iota((subs, rows_all), 1) % slots
    a_row = jnp.sum(jnp.where(slot_row == iota((subs, rows_all), 0), assign_col, 0), axis=0, keepdims=True)
    side_col = iota((rows_all, rows_all), 0) // slots % 2
    side_row = iota((rows_all, rows_all), 1) // slots % 2

    def plus(a, d):
        step = (4 * depth, depth, 1)[d]
        size = (4, 4, depth)[d]
        place = (a // step) % size
        return a + jnp.where(place == size - 1, step * (1 - size), step)

    for d in range(3):
        ahead = (plus(a_col, d) == a_row) & (side_col == 0) & (side_row == 1)
        behind = (a_col == plus(a_row, d)) & (side_col == 1) & (side_row == 0)
        perm[d] = jnp.where(ahead | behind, 1.0, 0.0).astype(BF16)

    lane_patch = iota((6, width), 1) // entries
    for l in range(slots):
        flags = solid_ref[l].astype(F32)
        mask = jnp.zeros((6, width), F32)
        for p in range(patches):
            mask = jnp.where(lane_patch == p, flags[:, p:p + 1], mask)
        smf[l] = mask
    for l in range(slots):
        for f in range(6):
            sm[row_of(l, f):row_of(l, f) + 1, :] = smf[l, f:f + 1, :]

    total = slots * nprim
    part_row = iota((total, coarse), 0)
    index = jnp.zeros((total, coarse), jnp.int32)
    for l in range(slots):
        for c in range(nprim // 3):
            index = jnp.where(part_row // 3 == l * (nprim // 3) + c, 3 * corners_ref[l, c], index)
    index = index + part_row % 3
    onehot[...] = jnp.where(index == iota((total, coarse), 1), 1.0, 0.0).astype(F32)

    def restrict(u, j, r, k):
        p = perm[u // tiles]
        rh, rl = split2(r)
        kh, kl = split2(k)
        moved = jnp.dot(p, jnp.concatenate([rh, rl, kh, kl], axis=1), preferred_element_type=F32)
        rp = moved[:, :LANES] + moved[:, LANES:2 * LANES]
        kp = moved[:, 2 * LANES:3 * LANES] + moved[:, 3 * LANES:]
        scale = 1.0 / (k + kp)
        w = k * scale
        wts[j, 0] = w
        wts[j, 1] = kp * scale
        return (w * (r + rp)).reshape(n, rows_unit, LANES)

    spread_wait(s1, rb1, rx1, 0)
    for j in range(base):
        tb2[:, j] = restrict(
            first(me) + j, j, rb1[:, j, 0].reshape(rows_all, LANES), rb1[:, j, 1].reshape(rows_all, LANES))
    if extra_any:
        @pl.when(has_extra(me))
        def _():
            tx2[...] = restrict(
                first(me) + base, base, rx1[:, 0].reshape(rows_all, LANES), rx1[:, 1].reshape(rows_all, LANES))
    back(tb2, tx2, b2, 1)
    basis_load.wait()
    back_wait(tb2, tx2, b2, 1)

    lane_group = iota((rows_unit, LANES), 1)
    for d in range(3):
        for ct in range(tiles):
            lanes = slice(ct * LANES, (ct + 1) * LANES)
            group = slice(d * rows_unit, (d + 1) * rows_unit)
            value = (sm[group, lanes] * b2[d * tiles + ct]).astype(BF16).astype(F32)
            for p in range(patches):
                keep = (lane_group + ct * LANES) // entries == p
                vt[p * rows_here + d * rows_unit:p * rows_here + (d + 1) * rows_unit, lanes] = jnp.where(keep, value, 0.0)
            for side in range(2):
                for l in range(slots):
                    xf[l, d + 3 * side:d + 3 * side + 1, lanes] = value[side * slots + l:side * slots + l + 1]

    parts = []
    for l in range(slots):
        acc = jnp.zeros((nprim, 6, LANES), F32)
        for ct in range(tiles):
            lanes = slice(ct * LANES, (ct + 1) * LANES)
            acc = acc + basis[l, :, :, lanes].astype(F32) * xf[l, :, lanes][None]
        parts.append(jnp.sum(acc, axis=1))
    part = jnp.sum(jnp.concatenate(parts, axis=0), axis=1, keepdims=True)
    ca_s[...] = jnp.sum(part * onehot[...], axis=0, keepdims=True)
    ca_r[me] = ca_s[...]
    each_sub(lambda k, p: small_sub(ca_s, ca_r, 0, k, p).start())

    vectors = vt[...].astype(BF16)
    columns = vectors.shape[0]
    sel[...] = jnp.zeros_like(sel)
    col_row = iota((entries, columns), 1) % rows_here

    def solve(l):
        inv_load[l].wait()
        result = lax.dot_general(
            inv[l].reshape(6 * entries, width), vectors, (((1,), (1,)), ((), ())), preferred_element_type=F32)
        total_sel = sel[0:entries, 0:columns]
        for f in range(6):
            total_sel = jnp.where(col_row == row_of(l, f), result[f * entries:(f + 1) * entries], total_sel)
        sel[0:entries, 0:columns] = total_sel

    half = (slots + 1) // 2
    for l in range(half):
        solve(l)
    each_sub(lambda k, p: small_sub_wait(ca_r, 0, p))
    cb_s[...] = jnp.sum(ca_r[...], axis=0)
    cb_r[mc] = cb_s[...]
    for k in range(1, m):
        small_crs(cb_s, cb_r, small_send.at[2], small_recv.at[2], k).start()
    for l in range(half, slots):
        solve(l)
    turned = sel[...].T
    for p in range(patches):
        loc[:, p * entries:(p + 1) * entries] = turned[p * rows_here:(p + 1) * rows_here, :entries]

    for k in range(1, m):
        small_crs_wait(ci, ci_send, ci_recv, k)
    for k in range(1, m):
        small_crs_wait(cb_r, small_send.at[2], small_recv.at[2], k)
    residual_row = jnp.sum(cb_r[...], axis=0)
    diagonal = iota((coarse, coarse), 0) == iota((coarse, coarse), 1)
    residual_col = jnp.sum(jnp.where(diagonal, residual_row, 0.0), axis=1, keepdims=True)
    coarse_solution = jnp.sum(residual_col * ci[...].reshape(coarse, coarse), axis=0, keepdims=True)
    values = jnp.sum(onehot[...] * coarse_solution, axis=1, keepdims=True)
    cv[...] = jnp.broadcast_to(values.astype(BF16).astype(F32), cv.shape)
    for l in range(slots):
        for ct in range(tiles):
            lanes = slice(ct * LANES, (ct + 1) * LANES)
            acc = jnp.zeros((6, LANES), F32)
            for c in range(nprim):
                at = l * nprim + c
                acc = acc + basis[l, c, :, lanes].astype(F32) * cv[at:at + 1, :]
            for f in range(6):
                corr[row_of(l, f):row_of(l, f) + 1, lanes] = acc[f:f + 1]

    inner = jnp.zeros((rows_unit, LANES), F32)
    for d in range(3):
        for ct in range(tiles):
            lanes = slice(ct * LANES, (ct + 1) * LANES)
            group = slice(d * rows_unit, (d + 1) * rows_unit)
            u = sm[group, lanes] * (loc[group, lanes] + corr[group, lanes])
            s3[d * tiles + ct] = u
            inner = inner + u * b2[d * tiles + ct]
    spread(s3, rb3, rx3, 2)
    ia_s[...] = jnp.sum(inner, axis=0, keepdims=True)
    ia_r[me] = ia_s[...]
    each_sub(lambda k, p: small_sub(ia_s, ia_r, 1, k, p).start())

    def average(u, j, x):
        xh, xl = split2(x)
        moved = jnp.dot(perm[u // tiles], jnp.concatenate([xh, xl], axis=1), preferred_element_type=F32)
        xp = moved[:, :LANES] + moved[:, LANES:]
        return (wts[j, 0] * x + wts[j, 1] * xp).reshape(n, rows_unit, LANES)

    spread_wait(s3, rb3, rx3, 2)
    for j in range(base):
        tb4[:, j] = average(first(me) + j, j, rb3[:, j].reshape(rows_all, LANES))
    if extra_any:
        @pl.when(has_extra(me))
        def _():
            tx4[...] = average(first(me) + base, base, rx3[...].reshape(rows_all, LANES))
    back(tb4, tx4, b4, 3)
    each_sub(lambda k, p: small_sub_wait(ia_r, 1, p))
    ib_s[...] = jnp.sum(ia_r[...], axis=0)
    ib_r[mc] = ib_s[...]
    for k in range(1, m):
        small_crs(ib_s, ib_r, small_send.at[3], small_recv.at[3], k).start()

    spread_done(s1, rb1, rx1, 0)
    back_done(tb2, tx2, b2, 1)
    spread_done(s3, rb3, rx3, 2)
    for k in range(1, m):
        small_crs(ci_ref, ci, ci_send, ci_recv, k).wait_send()
        small_crs(cb_s, cb_r, small_send.at[2], small_recv.at[2], k).wait_send()
    each_sub(lambda k, p: small_sub(ca_s, ca_r, 0, k, p).wait_send())
    each_sub(lambda k, p: small_sub(ia_s, ia_r, 1, k, p).wait_send())

    back_wait(tb4, tx4, b4, 3)
    for l in range(slots):
        for f in range(6):
            for ct in range(tiles):
                row = (f // 3) * slots + l
                out_ref[l, f:f + 1, ct * LANES:(ct + 1) * LANES] = b4[(f % 3) * tiles + ct, row:row + 1, :]
    for k in range(1, m):
        small_crs_wait(ib_r, small_send.at[3], small_recv.at[3], k)
    inner_ref[...] = jnp.sum(jnp.sum(ib_r[...], axis=0), axis=1, keepdims=True)
    back_done(tb4, tx4, b4, 3)
    for k in range(1, m):
        small_crs(ib_s, ib_r, small_send.at[3], small_recv.at[3], k).wait_send()


def body(residual, stiffness, solid, inverses, coarse_basis, assign, corners, coarse_inverse):
    slots, faces, width = residual.shape
    patches = solid.shape[2]
    entries = width // patches
    n, m = lax.axis_size("sub"), lax.axis_size("crs")
    subs = assign.shape[0]
    tiles = width // LANES
    units = 3 * tiles
    base = units // n
    rows = 2 * slots
    rows_all = n * rows
    nprim = coarse_basis.shape[1]
    coarse = coarse_inverse.shape[1]
    cfg = (n, m, slots, tiles, patches, entries, subs)
    kept = max(base, 1)
    vt_rows = -(-(patches * rows * 3) // LANES) * LANES if patches * rows * 3 > LANES else patches * rows * 3
    square = -(-entries // LANES) * LANES
    lanes_sel = -(-vt_rows // LANES) * LANES
    vmem = pl.BlockSpec(memory_space=pltpu.VMEM)
    smem = pl.BlockSpec(memory_space=pltpu.SMEM)
    anyw = pl.BlockSpec(memory_space=pl.ANY)
    size = max(n, m)
    out, inner = pl.pallas_call(
        functools.partial(kernel, cfg),
        out_shape=(
            jax.ShapeDtypeStruct(residual.shape, F32),
            jax.ShapeDtypeStruct((1, 1), F32),
        ),
        in_specs=[vmem, vmem, vmem, anyw, anyw, vmem, smem, vmem],
        out_specs=(vmem, vmem),
        scratch_shapes=[
            pltpu.VMEM(inverses.shape, BF16),
            pltpu.VMEM(coarse_basis.shape, BF16),
            pltpu.VMEM((units, 2, rows, LANES), F32),
            pltpu.VMEM((n, kept, 2, rows, LANES), F32),
            pltpu.VMEM((n, 2, rows, LANES), F32),
            pltpu.VMEM((base + 1, 2, rows_all, LANES), F32),
            pltpu.VMEM((n, kept, rows, LANES), F32),
            pltpu.VMEM((n, rows, LANES), F32),
            pltpu.VMEM((units, rows, LANES), F32),
            pltpu.VMEM((units, rows, LANES), F32),
            pltpu.VMEM((n, kept, rows, LANES), F32),
            pltpu.VMEM((n, rows, LANES), F32),
            pltpu.VMEM((n, kept, rows, LANES), F32),
            pltpu.VMEM((n, rows, LANES), F32),
            pltpu.VMEM((units, rows, LANES), F32),
            pltpu.VMEM((3, rows_all, rows_all), BF16),
            pltpu.VMEM((slots, 6, width), F32),
            pltpu.VMEM((3 * rows, width), F32),
            pltpu.VMEM((slots, 6, width), F32),
            pltpu.VMEM((3 * rows, width), F32),
            pltpu.VMEM((3 * rows, width), F32),
            pltpu.VMEM((vt_rows, width), F32),
            pltpu.VMEM((square, lanes_sel), F32),
            pltpu.VMEM((slots * nprim, coarse), F32),
            pltpu.VMEM((slots * nprim, LANES), F32),
            pltpu.VMEM((m,) + coarse_inverse.shape, F32),
            pltpu.VMEM((1, coarse), F32),
            pltpu.VMEM((n, 1, coarse), F32),
            pltpu.VMEM((1, coarse), F32),
            pltpu.VMEM((m, 1, coarse), F32),
            pltpu.VMEM((1, LANES), F32),
            pltpu.VMEM((n, 1, LANES), F32),
            pltpu.VMEM((1, LANES), F32),
            pltpu.VMEM((m, 1, LANES), F32),
            pltpu.SemaphoreType.DMA((4, 2, n)),
            pltpu.SemaphoreType.DMA((4, 2, n)),
            pltpu.SemaphoreType.DMA((4, 2)),
            pltpu.SemaphoreType.DMA((slots + 1,)),
            pltpu.SemaphoreType.DMA((4, size)),
            pltpu.SemaphoreType.DMA((4, size)),
            pltpu.SemaphoreType.DMA((m,)),
            pltpu.SemaphoreType.DMA((m,)),
        ],
        compiler_params=pltpu.CompilerParams(
            collective_id=0, has_side_effects=True, vmem_limit_bytes=40 * 1024 * 1024
        ),
    )(residual, stiffness, solid, inverses, coarse_basis, assign.reshape(1, subs), corners, coarse_inverse)
    return out, inner.reshape(1)


def solution(mesh):
    return jax.shard_map(
        body,
        mesh=mesh,
        in_specs=(
            P("sub", None, "crs"),
            P("sub", None, "crs"),
            P("sub", None, "crs"),
            P("sub", None, None, "crs"),
            P("sub", None, None, "crs"),
            P(),
            P("sub", None),
            P("crs", None),
        ),
        out_specs=(P("sub", None, "crs"), P()),
        check_vma=False,
    )
```

```python
import functools

import jax
import jax.numpy as jnp
from jax import lax
from jax.experimental import pallas as pl
from jax.experimental.pallas import tpu as pltpu
from jax.sharding import PartitionSpec as P

F32 = jnp.float32
BF16 = jnp.bfloat16
LANES = 128


def iota(shape, dim):
    return lax.broadcasted_iota(jnp.int32, shape, dim)


def split2(x):
    high = x.astype(BF16)
    low = (x - high.astype(F32)).astype(BF16)
    return high, low


def kernel(
    cfg,
    r_hbm, k_hbm, solid_hbm, inv_hbm, basis_hbm, assign_hbm, corners_hbm, ci_hbm,
    out_ref, inner_ref,
    r_ref, k_ref, solid_ref, assign_ref, corners_ref, ci_ref,
    inv, basis, faces_basis, s1, rb1, rx1, wts, tb2, tx2, b2, s3, rb3, rx3, tb4, tx4, b4,
    perm, sm, loc, corr, vt, vectors_ref, sel, onehot, onehot_t, ci, ci_t,
    ca_s, ca_r, cb_s, cb_r, ia_s, ia_r, ib_s, ib_r,
    send, recv, own, load, small_load, small_send, small_recv, ci_send, ci_recv,
):
    n, m, slots, tiles, patches, entries, subs = cfg
    depth = subs // 16
    units = 3 * tiles
    base = units // n
    extra_any = units % n != 0
    rows_unit = 2 * slots
    rows_all = n * rows_unit
    rows_here = 6 * slots
    width = tiles * LANES
    nprim = basis.shape[2]
    coarse = ci_ref.shape[1]
    me = lax.axis_index("sub")
    mc = lax.axis_index("crs")

    def first(p):
        return (p * units + n - 1) // n

    def has_extra(p):
        return first(p + 1) - first(p) > base

    def row_of(l, f):
        return (f % 3) * rows_unit + (f // 3) * slots + l

    small = [
        pltpu.make_async_copy(src, dst, small_load.at[i])
        for i, (src, dst) in enumerate((
            (r_hbm, r_ref), (k_hbm, k_ref), (ci_hbm, ci_ref), (assign_hbm, assign_ref),
            (solid_hbm, solid_ref), (corners_hbm, corners_ref)))
    ]
    for c in small:
        c.start()
    basis_load = pltpu.make_async_copy(basis_hbm, basis, load.at[slots])
    basis_load.start()
    inv_load = [pltpu.make_async_copy(inv_hbm.at[l], inv.at[l], load.at[l]) for l in range(slots)]
    for c in inv_load:
        c.start()

    def each_sub(body):
        if n <= 8:
            for k in range(1, n):
                body(k, lax.rem(me + k, n))
        else:
            def step(k, carry):
                body(k, lax.rem(me + k, n))
                return carry
            lax.fori_loop(1, n, step, 0)

    barrier = pltpu.get_barrier_semaphore()

    def greet(k, p):
        pl.semaphore_signal(barrier, inc=1, device_id={"sub": p}, device_id_type=pl.DeviceIdType.MESH)

    each_sub(greet)
    for k in range(1, m):
        pl.semaphore_signal(barrier, inc=1, device_id={"crs": lax.rem(mc + k, m)}, device_id_type=pl.DeviceIdType.MESH)

    for a, ref in enumerate((r_ref, k_ref)):
        small[a].wait()
        for f in range(6):
            for ct in range(tiles):
                row = (f // 3) * slots
                s1[(f % 3) * tiles + ct, a, row:row + slots, :] = ref[f, :, ct * LANES:(ct + 1) * LANES]

    def to_sub(src, dst, stage, kind, k, p):
        return pltpu.make_async_remote_copy(
            src_ref=src, dst_ref=dst, send_sem=send.at[stage, kind, k], recv_sem=recv.at[stage, kind, me],
            device_id={"sub": p}, device_id_type=pl.DeviceIdType.MESH)

    def from_sub(dst, stage, kind, p):
        pltpu.make_async_remote_copy(
            src_ref=dst, dst_ref=dst, send_sem=send.at[stage, kind, 0], recv_sem=recv.at[stage, kind, p],
            device_id={"sub": p}, device_id_type=pl.DeviceIdType.MESH).wait_recv()

    def spread(src, dst_base, dst_extra, stage):
        def go(k, p):
            if base:
                to_sub(src.at[pl.ds(first(p), base)], dst_base.at[me], stage, 0, k, p).start()
            if extra_any:
                @pl.when(has_extra(p))
                def _():
                    to_sub(src.at[first(p) + base], dst_extra.at[me], stage, 1, k, p).start()
        each_sub(go)
        if base:
            pltpu.make_async_copy(src.at[pl.ds(first(me), base)], dst_base.at[me], own.at[stage, 0]).start()
        if extra_any:
            @pl.when(has_extra(me))
            def _():
                pltpu.make_async_copy(src.at[first(me) + base], dst_extra.at[me], own.at[stage, 1]).start()

    def spread_wait(src, dst_base, dst_extra, stage):
        if base:
            pltpu.make_async_copy(src.at[pl.ds(first(me), base)], dst_base.at[me], own.at[stage, 0]).wait()
            each_sub(lambda k, p: from_sub(dst_base.at[p], stage, 0, p))
        if extra_any:
            @pl.when(has_extra(me))
            def _():
                pltpu.make_async_copy(src.at[first(me) + base], dst_extra.at[me], own.at[stage, 1]).wait()
                each_sub(lambda k, p: from_sub(dst_extra.at[p], stage, 1, p))

    def spread_done(src, dst_base, dst_extra, stage):
        def go(k, p):
            if base:
                to_sub(src.at[pl.ds(first(p), base)], dst_base.at[me], stage, 0, k, p).wait_send()
            if extra_any:
                @pl.when(has_extra(p))
                def _():
                    to_sub(src.at[first(p) + base], dst_extra.at[me], stage, 1, k, p).wait_send()
        each_sub(go)

    def back(src_base, src_extra, dst, stage):
        def go(k, p):
            if base:
                to_sub(src_base.at[p], dst.at[pl.ds(first(me), base)], stage, 0, k, p).start()
        each_sub(go)
        if base:
            pltpu.make_async_copy(src_base.at[me], dst.at[pl.ds(first(me), base)], own.at[stage, 0]).start()
        if extra_any:
            @pl.when(has_extra(me))
            def _():
                each_sub(lambda k, p: to_sub(src_extra.at[p], dst.at[first(me) + base], stage, 1, k, p).start())
                pltpu.make_async_copy(src_extra.at[me], dst.at[first(me) + base], own.at[stage, 1]).start()

    def back_wait(src_base, src_extra, dst, stage):
        if base:
            pltpu.make_async_copy(src_base.at[me], dst.at[pl.ds(first(me), base)], own.at[stage, 0]).wait()
        if extra_any:
            @pl.when(has_extra(me))
            def _():
                pltpu.make_async_copy(src_extra.at[me], dst.at[first(me) + base], own.at[stage, 1]).wait()

        def go(k, p):
            if base:
                from_sub(dst.at[pl.ds(first(p), base)], stage, 0, p)
            if extra_any:
                @pl.when(has_extra(p))
                def _():
                    from_sub(dst.at[first(p) + base], stage, 1, p)
        each_sub(go)

    def back_done(src_base, src_extra, dst, stage):
        if base:
            each_sub(lambda k, p: to_sub(src_base.at[p], dst.at[pl.ds(first(me), base)], stage, 0, k, p).wait_send())
        if extra_any:
            @pl.when(has_extra(me))
            def _():
                each_sub(lambda k, p: to_sub(src_extra.at[p], dst.at[first(me) + base], stage, 1, k, p).wait_send())

    def small_sub(src, dst, which, k, p):
        return pltpu.make_async_remote_copy(
            src_ref=src, dst_ref=dst.at[me], send_sem=small_send.at[which, k], recv_sem=small_recv.at[which, me],
            device_id={"sub": p}, device_id_type=pl.DeviceIdType.MESH)

    def small_sub_wait(dst, which, p):
        pltpu.make_async_remote_copy(
            src_ref=dst.at[p], dst_ref=dst.at[p], send_sem=small_send.at[which, 0], recv_sem=small_recv.at[which, p],
            device_id={"sub": p}, device_id_type=pl.DeviceIdType.MESH).wait_recv()

    def small_crs(src, dst, send_sem, recv_sem, k):
        return pltpu.make_async_remote_copy(
            src_ref=src, dst_ref=dst.at[mc], send_sem=send_sem.at[k], recv_sem=recv_sem.at[mc],
            device_id={"crs": lax.rem(mc + k, m)}, device_id_type=pl.DeviceIdType.MESH)

    def small_crs_wait(dst, send_sem, recv_sem, k):
        q = lax.rem(mc + k, m)
        pltpu.make_async_remote_copy(
            src_ref=dst.at[q], dst_ref=dst.at[q], send_sem=send_sem.at[0], recv_sem=recv_sem.at[q],
            device_id={"crs": q}, device_id_type=pl.DeviceIdType.MESH).wait_recv()

    pl.semaphore_wait(barrier, n - 1 + m - 1)
    spread(s1, rb1, rx1, 0)
    for c in small[2:]:
        c.wait()
    for k in range(1, m):
        small_crs(ci_ref, ci, ci_send, ci_recv, k).start()

    ci[mc] = ci_ref[...]
    assign_row = assign_ref[...]
    pick = iota((subs, subs), 0) == iota((subs, subs), 1)
    assign_col = jnp.sum(jnp.where(pick, assign_row, 0), axis=1, keepdims=True)
    slot_col = iota((rows_all, 1), 0) // rows_unit * slots + iota((rows_all, 1), 0) % slots
    a_col = jnp.sum(jnp.where(slot_col == iota((rows_all, subs), 1), assign_row, 0), axis=1, keepdims=True)
    slot_row = iota((1, rows_all), 1) // rows_unit * slots + iota((1, rows_all), 1) % slots
    a_row = jnp.sum(jnp.where(slot_row == iota((subs, rows_all), 0), assign_col, 0), axis=0, keepdims=True)
    side_col = iota((rows_all, 1), 0) // slots % 2
    side_row = iota((1, rows_all), 1) // slots % 2

    def plus(a, d):
        step = (4 * depth, depth, 1)[d]
        size = (4, 4, depth)[d]
        place = (a // step) % size
        return a + jnp.where(place == size - 1, step * (1 - size), step)

    for d in range(3):
        ahead = (plus(a_col, d) == a_row) & (side_col == 0) & (side_row == 1)
        behind = (a_col == plus(a_row, d)) & (side_col == 1) & (side_row == 0)
        perm[d] = jnp.where(ahead | behind, 1.0, 0.0).astype(BF16)

    lane = iota((1, LANES), 1)
    for p in range(patches):
        flags = solid_ref[:, p, :].astype(F32)
        for f in range(6):
            flag = flags[:, f:f + 1]
            at = row_of(0, f)
            for ct in range(tiles):
                low, high = p * entries - ct * LANES, (p + 1) * entries - ct * LANES
                if low >= LANES or high <= 0:
                    continue
                lanes = slice(ct * LANES, (ct + 1) * LANES)
                if low <= 0:
                    sm[at:at + slots, lanes] = jnp.broadcast_to(flag, (slots, LANES))
                else:
                    sm[at:at + slots, lanes] = jnp.where(lane >= low, flag, sm[at:at + slots, lanes])

    total = slots * nprim
    ncorner = nprim // 3
    part_col = iota((total, 1), 0)
    group = part_col // 3
    index = jnp.zeros((total, ncorner), jnp.int32)
    for l in range(slots):
        index = jnp.where(group == l * ncorner + iota((1, ncorner), 1), corners_ref[l:l + 1, :], index)
    index = 3 * jnp.sum(index, axis=1, keepdims=True) + part_col % 3
    hot = jnp.where(index == iota((total, coarse), 1), 1.0, 0.0).astype(F32)
    onehot[...] = hot
    onehot_t[...] = hot.T
    vt[...] = jnp.zeros_like(vt)
    col_row = iota((1, vt.shape[0]), 1) % rows_here
    sel[...] = jnp.zeros_like(sel)

    basis_load.wait()
    for f in range(6):
        faces_basis[f] = jnp.concatenate(
            [basis[l, f].astype(F32) for l in range(slots)], axis=0).astype(BF16)

    def restrict(u, j, r, k):
        p = perm[u // tiles]
        rh, rl = split2(r)
        kh, kl = split2(k)
        moved = jnp.dot(p, jnp.concatenate([rh, rl, kh, kl], axis=1), preferred_element_type=F32)
        rp = moved[:, :LANES] + moved[:, LANES:2 * LANES]
        kp = moved[:, 2 * LANES:3 * LANES] + moved[:, 3 * LANES:]
        scale = 1.0 / (k + kp)
        w = k * scale
        wts[j, 0] = w
        wts[j, 1] = kp * scale
        return (w * (r + rp)).reshape(n, rows_unit, LANES)

    spread_wait(s1, rb1, rx1, 0)
    for j in range(base):
        tb2[:, j] = restrict(
            first(me) + j, j, rb1[:, j, 0].reshape(rows_all, LANES), rb1[:, j, 1].reshape(rows_all, LANES))
    if extra_any:
        @pl.when(has_extra(me))
        def _():
            tx2[...] = restrict(
                first(me) + base, base, rx1[:, 0].reshape(rows_all, LANES), rx1[:, 1].reshape(rows_all, LANES))
    back(tb2, tx2, b2, 1)
    for k in range(1, m):
        small_crs_wait(ci, ci_send, ci_recv, k)
    ci_t[...] = ci[...].reshape(coarse, coarse).T
    back_wait(tb2, tx2, b2, 1)

    for d in range(3):
        for ct in range(tiles):
            lanes = slice(ct * LANES, (ct + 1) * LANES)
            group = slice(d * rows_unit, (d + 1) * rows_unit)
            value = sm[group, lanes] * b2[d * tiles + ct]
            for p in range(patches):
                low, high = p * entries - ct * LANES, (p + 1) * entries - ct * LANES
                if low >= LANES or high <= 0:
                    continue
                kept = value
                if low > 0:
                    kept = jnp.where(lane >= low, kept, 0.0)
                if high < LANES:
                    kept = jnp.where(lane < high, kept, 0.0)
                at = p * rows_here + d * rows_unit
                vt[at:at + rows_unit, lanes] = kept
    for ct in range(tiles):
        lanes = slice(ct * LANES, (ct + 1) * LANES)
        vectors_ref[lanes, :] = vt[:, lanes].T.astype(BF16)
    vectors = vectors_ref[...]
    columns = vectors.shape[1]

    products = jnp.dot(faces_basis[...].reshape(6 * total, width), vectors, preferred_element_type=F32)
    parts = []
    for l in range(slots):
        acc = jnp.zeros((nprim, columns), F32)
        for f in range(6):
            at = f * total + l * nprim
            acc = jnp.where(col_row == row_of(l, f), products[at:at + nprim], 0.0) + acc
        parts.append(acc)
    part = jnp.sum(jnp.concatenate(parts, axis=0), axis=1, keepdims=True)
    ca_s[...] = jnp.sum(part * onehot[...], axis=0, keepdims=True)
    ca_r[me] = ca_s[...]
    each_sub(lambda k, p: small_sub(ca_s, ca_r, 0, k, p).start())

    def solve(l):
        inv_load[l].wait()
        result = jnp.dot(inv[l].reshape(6 * entries, width), vectors, preferred_element_type=F32)
        total_sel = sel[0:entries, 0:columns]
        for f in range(6):
            total_sel = jnp.where(col_row == row_of(l, f), result[f * entries:(f + 1) * entries], total_sel)
        sel[0:entries, 0:columns] = total_sel

    half = (slots + 1) // 2
    for l in range(half):
        solve(l)
    each_sub(lambda k, p: small_sub_wait(ca_r, 0, p))
    cb_s[...] = jnp.sum(ca_r[...], axis=0)
    cb_r[mc] = cb_s[...]
    for k in range(1, m):
        small_crs(cb_s, cb_r, small_send.at[2], small_recv.at[2], k).start()
    for l in range(half, slots):
        solve(l)
    turned = sel[...].T
    for p in range(patches):
        loc[:, p * entries:(p + 1) * entries] = turned[p * rows_here:(p + 1) * rows_here, :entries]

    for k in range(1, m):
        small_crs_wait(cb_r, small_send.at[2], small_recv.at[2], k)
    residual_row = jnp.sum(cb_r[...], axis=0)
    coarse_solution = jnp.sum(ci_t[...] * residual_row, axis=1, keepdims=True)
    values = jnp.sum(onehot_t[...] * coarse_solution, axis=0, keepdims=True)
    slot_at = iota((rows_unit, 1), 0) % slots * nprim
    place = iota((1, total), 1)
    corner_values = jnp.where((place >= slot_at) & (place < slot_at + nprim), values, 0.0).astype(BF16)
    near = iota((rows_unit, 1), 0) < slots
    for d in range(3):
        corr[d * rows_unit:(d + 1) * rows_unit, :] = jnp.where(
            near,
            jnp.dot(corner_values, faces_basis[d], preferred_element_type=F32),
            jnp.dot(corner_values, faces_basis[d + 3], preferred_element_type=F32))

    inner = jnp.zeros((rows_unit, LANES), F32)
    for d in range(3):
        for ct in range(tiles):
            lanes = slice(ct * LANES, (ct + 1) * LANES)
            group = slice(d * rows_unit, (d + 1) * rows_unit)
            u = sm[group, lanes] * (loc[group, lanes] + corr[group, lanes])
            s3[d * tiles + ct] = u
            inner = inner + u * b2[d * tiles + ct]
    spread(s3, rb3, rx3, 2)
    ia_s[...] = jnp.sum(inner, axis=0, keepdims=True)
    ia_r[me] = ia_s[...]
    each_sub(lambda k, p: small_sub(ia_s, ia_r, 1, k, p).start())

    def average(u, j, x):
        xh, xl = split2(x)
        moved = jnp.dot(perm[u // tiles], jnp.concatenate([xh, xl], axis=1), preferred_element_type=F32)
        xp = moved[:, :LANES] + moved[:, LANES:]
        return (wts[j, 0] * x + wts[j, 1] * xp).reshape(n, rows_unit, LANES)

    spread_wait(s3, rb3, rx3, 2)
    for j in range(base):
        tb4[:, j] = average(first(me) + j, j, rb3[:, j].reshape(rows_all, LANES))
    if extra_any:
        @pl.when(has_extra(me))
        def _():
            tx4[...] = average(first(me) + base, base, rx3[...].reshape(rows_all, LANES))
    back(tb4, tx4, b4, 3)
    each_sub(lambda k, p: small_sub_wait(ia_r, 1, p))
    ib_s[...] = jnp.sum(ia_r[...], axis=0)
    ib_r[mc] = ib_s[...]
    for k in range(1, m):
        small_crs(ib_s, ib_r, small_send.at[3], small_recv.at[3], k).start()

    spread_done(s1, rb1, rx1, 0)
    back_done(tb2, tx2, b2, 1)
    spread_done(s3, rb3, rx3, 2)
    for k in range(1, m):
        small_crs(ci_ref, ci, ci_send, ci_recv, k).wait_send()
        small_crs(cb_s, cb_r, small_send.at[2], small_recv.at[2], k).wait_send()
    each_sub(lambda k, p: small_sub(ca_s, ca_r, 0, k, p).wait_send())
    each_sub(lambda k, p: small_sub(ia_s, ia_r, 1, k, p).wait_send())

    back_wait(tb4, tx4, b4, 3)
    for f in range(6):
        for ct in range(tiles):
            row = (f // 3) * slots
            out_ref[f, :, ct * LANES:(ct + 1) * LANES] = b4[(f % 3) * tiles + ct, row:row + slots, :]
    for k in range(1, m):
        small_crs_wait(ib_r, small_send.at[3], small_recv.at[3], k)
    inner_ref[...] = jnp.sum(jnp.sum(ib_r[...], axis=0), axis=1, keepdims=True)
    back_done(tb4, tx4, b4, 3)
    for k in range(1, m):
        small_crs(ib_s, ib_r, small_send.at[3], small_recv.at[3], k).wait_send()


def body(residual, stiffness, solid, inverses, coarse_basis, assign, corners, coarse_inverse):
    slots, faces, width = residual.shape
    patches = solid.shape[2]
    entries = width // patches
    n, m = lax.axis_size("sub"), lax.axis_size("crs")
    subs = assign.shape[0]
    tiles = width // LANES
    units = 3 * tiles
    base = units // n
    rows = 2 * slots
    rows_all = n * rows
    nprim = coarse_basis.shape[1]
    coarse = coarse_inverse.shape[1]
    cfg = (n, m, slots, tiles, patches, entries, subs)
    kept = max(base, 1)
    vt_rows = -(-(patches * rows * 3) // LANES) * LANES
    square = -(-entries // LANES) * LANES
    vmem = pl.BlockSpec(memory_space=pltpu.VMEM)
    anyw = pl.BlockSpec(memory_space=pl.ANY)
    size = max(n, m)
    out, inner = pl.pallas_call(
        functools.partial(kernel, cfg),
        out_shape=(
            jax.ShapeDtypeStruct((faces, slots, width), F32),
            jax.ShapeDtypeStruct((1, 1), F32),
        ),
        in_specs=[anyw] * 8,
        out_specs=(vmem, vmem),
        scratch_shapes=[
            pltpu.VMEM((faces, slots, width), F32),
            pltpu.VMEM((faces, slots, width), F32),
            pltpu.VMEM((slots, patches, faces), jnp.int32),
            pltpu.VMEM((1, subs), jnp.int32),
            pltpu.VMEM(corners.shape, jnp.int32),
            pltpu.VMEM(coarse_inverse.shape, F32),
            pltpu.VMEM(inverses.shape, BF16),
            pltpu.VMEM((slots, faces, nprim, width), BF16),
            pltpu.VMEM((faces, slots * nprim, width), BF16),
            pltpu.VMEM((units, 2, rows, LANES), F32),
            pltpu.VMEM((n, kept, 2, rows, LANES), F32),
            pltpu.VMEM((n, 2, rows, LANES), F32),
            pltpu.VMEM((base + 1, 2, rows_all, LANES), F32),
            pltpu.VMEM((n, kept, rows, LANES), F32),
            pltpu.VMEM((n, rows, LANES), F32),
            pltpu.VMEM((units, rows, LANES), F32),
            pltpu.VMEM((units, rows, LANES), F32),
            pltpu.VMEM((n, kept, rows, LANES), F32),
            pltpu.VMEM((n, rows, LANES), F32),
            pltpu.VMEM((n, kept, rows, LANES), F32),
            pltpu.VMEM((n, rows, LANES), F32),
            pltpu.VMEM((units, rows, LANES), F32),
            pltpu.VMEM((3, rows_all, rows_all), BF16),
            pltpu.VMEM((3 * rows, width), F32),
            pltpu.VMEM((3 * rows, width), F32),
            pltpu.VMEM((3 * rows, width), F32),
            pltpu.VMEM((vt_rows, width), F32),
            pltpu.VMEM((width, vt_rows), BF16),
            pltpu.VMEM((square, vt_rows), F32),
            pltpu.VMEM((slots * nprim, coarse), F32),
            pltpu.VMEM((coarse, slots * nprim), F32),
            pltpu.VMEM((m,) + coarse_inverse.shape, F32),
            pltpu.VMEM((coarse, coarse), F32),
            pltpu.VMEM((1, coarse), F32),
            pltpu.VMEM((n, 1, coarse), F32),
            pltpu.VMEM((1, coarse), F32),
            pltpu.VMEM((m, 1, coarse), F32),
            pltpu.VMEM((1, LANES), F32),
            pltpu.VMEM((n, 1, LANES), F32),
            pltpu.VMEM((1, LANES), F32),
            pltpu.VMEM((m, 1, LANES), F32),
            pltpu.SemaphoreType.DMA((4, 2, n)),
            pltpu.SemaphoreType.DMA((4, 2, n)),
            pltpu.SemaphoreType.DMA((4, 2)),
            pltpu.SemaphoreType.DMA((slots + 1,)),
            pltpu.SemaphoreType.DMA((6,)),
            pltpu.SemaphoreType.DMA((4, size)),
            pltpu.SemaphoreType.DMA((4, size)),
            pltpu.SemaphoreType.DMA((m,)),
            pltpu.SemaphoreType.DMA((m,)),
        ],
        compiler_params=pltpu.CompilerParams(
            collective_id=0, has_side_effects=True, vmem_limit_bytes=60 * 1024 * 1024
        ),
    )(
        residual.transpose(1, 0, 2), stiffness.transpose(1, 0, 2), solid.transpose(0, 2, 1), inverses,
        coarse_basis.transpose(0, 2, 1, 3), assign.reshape(1, subs), corners, coarse_inverse)
    return out.transpose(1, 0, 2), inner.reshape(1)


def solution(mesh):
    return jax.shard_map(
        body,
        mesh=mesh,
        in_specs=(
            P("sub", None, "crs"),
            P("sub", None, "crs"),
            P("sub", None, "crs"),
            P("sub", None, None, "crs"),
            P("sub", None, None, "crs"),
            P(),
            P("sub", None),
            P("crs", None),
        ),
        out_specs=(P("sub", None, "crs"), P()),
        check_vma=False,
    )
```

```python
import functools

import jax
import jax.numpy as jnp
from jax import lax
from jax.experimental import pallas as pl
from jax.experimental.pallas import tpu as pltpu
from jax.sharding import PartitionSpec as P

F32 = jnp.float32
BF16 = jnp.bfloat16
LANES = 128


def iota(shape, dim):
    return lax.broadcasted_iota(jnp.int32, shape, dim)


def split2(x):
    high = x.astype(BF16)
    low = (x - high.astype(F32)).astype(BF16)
    return high, low


def kernel(
    cfg,
    r_hbm, k_hbm, solid_hbm, inv_hbm, basis_hbm, assign_hbm, corners_hbm, ci_hbm,
    out_ref, inner_ref,
    r_ref, k_ref, solid_ref, assign_ref, corners_ref, ci_ref,
    inv, basis, faces_basis, s1, rb1, rx1, wts, tb2, tx2, b2, s3, rb3, rx3, tb4, tx4, b4,
    perm, sm, loc, corr, vt, vectors_ref, sel, onehot, onehot_t, ci, ci_t,
    ca_s, ca_r, cb_s, cb_r, ia_s, ia_r, ib_s, ib_r,
    send, recv, own, load, small_load, small_send, small_recv, ci_send, ci_recv,
):
    n, m, slots, tiles, patches, entries, subs = cfg
    depth = subs // 16
    units = 3 * tiles
    base = units // n
    extra_any = units % n != 0
    rows_unit = 2 * slots
    rows_all = n * rows_unit
    rows_here = 6 * slots
    width = tiles * LANES
    nprim = basis.shape[2]
    coarse = ci_ref.shape[1]
    me = lax.axis_index("sub")
    mc = lax.axis_index("crs")

    def first(p):
        return (p * units + n - 1) // n

    def has_extra(p):
        return first(p + 1) - first(p) > base

    def row_of(l, f):
        return (f % 3) * rows_unit + (f // 3) * slots + l

    small = [
        pltpu.make_async_copy(src, dst, small_load.at[i])
        for i, (src, dst) in enumerate((
            (r_hbm, r_ref), (k_hbm, k_ref), (ci_hbm, ci_ref), (assign_hbm, assign_ref),
            (solid_hbm, solid_ref), (corners_hbm, corners_ref)))
    ]
    for c in small:
        c.start()
    basis_load = pltpu.make_async_copy(basis_hbm, basis, load.at[slots])
    basis_load.start()
    inv_load = [pltpu.make_async_copy(inv_hbm.at[l], inv.at[l], load.at[l]) for l in range(slots)]
    for c in inv_load:
        c.start()

    def each_sub(body):
        if n <= 8:
            for k in range(1, n):
                body(k, lax.rem(me + k, n))
        else:
            def step(k, carry):
                body(k, lax.rem(me + k, n))
                return carry
            lax.fori_loop(1, n, step, 0)

    barrier = pltpu.get_barrier_semaphore()

    def greet(k, p):
        pl.semaphore_signal(barrier, inc=1, device_id={"sub": p}, device_id_type=pl.DeviceIdType.MESH)

    each_sub(greet)
    for k in range(1, m):
        pl.semaphore_signal(barrier, inc=1, device_id={"crs": lax.rem(mc + k, m)}, device_id_type=pl.DeviceIdType.MESH)

    for a, ref in enumerate((r_ref, k_ref)):
        small[a].wait()
        for f in range(6):
            for ct in range(tiles):
                row = (f // 3) * slots
                s1[(f % 3) * tiles + ct, a, row:row + slots, :] = ref[f, :, ct * LANES:(ct + 1) * LANES]

    def to_sub(src, dst, stage, kind, k, p):
        return pltpu.make_async_remote_copy(
            src_ref=src, dst_ref=dst, send_sem=send.at[stage, kind, k], recv_sem=recv.at[stage, kind, me],
            device_id={"sub": p}, device_id_type=pl.DeviceIdType.MESH)

    def from_sub(dst, stage, kind, p):
        pltpu.make_async_remote_copy(
            src_ref=dst, dst_ref=dst, send_sem=send.at[stage, kind, 0], recv_sem=recv.at[stage, kind, p],
            device_id={"sub": p}, device_id_type=pl.DeviceIdType.MESH).wait_recv()

    def spread(src, dst_base, dst_extra, stage):
        def go(k, p):
            if base:
                to_sub(src.at[pl.ds(first(p), base)], dst_base.at[me], stage, 0, k, p).start()
            if extra_any:
                @pl.when(has_extra(p))
                def _():
                    to_sub(src.at[first(p) + base], dst_extra.at[me], stage, 1, k, p).start()
        each_sub(go)
        if base:
            pltpu.make_async_copy(src.at[pl.ds(first(me), base)], dst_base.at[me], own.at[stage, 0]).start()
        if extra_any:
            @pl.when(has_extra(me))
            def _():
                pltpu.make_async_copy(src.at[first(me) + base], dst_extra.at[me], own.at[stage, 1]).start()

    def spread_wait(src, dst_base, stage):
        if base:
            pltpu.make_async_copy(src.at[pl.ds(first(me), base)], dst_base.at[me], own.at[stage, 0]).wait()
            each_sub(lambda k, p: from_sub(dst_base.at[p], stage, 0, p))

    def spread_wait_extra(src, dst_extra, stage):
        pltpu.make_async_copy(src.at[first(me) + base], dst_extra.at[me], own.at[stage, 1]).wait()
        each_sub(lambda k, p: from_sub(dst_extra.at[p], stage, 1, p))

    def spread_done(src, dst_base, dst_extra, stage):
        def go(k, p):
            if base:
                to_sub(src.at[pl.ds(first(p), base)], dst_base.at[me], stage, 0, k, p).wait_send()
            if extra_any:
                @pl.when(has_extra(p))
                def _():
                    to_sub(src.at[first(p) + base], dst_extra.at[me], stage, 1, k, p).wait_send()
        each_sub(go)

    def back(src_base, dst, stage):
        def go(k, p):
            if base:
                to_sub(src_base.at[p], dst.at[pl.ds(first(me), base)], stage, 0, k, p).start()
        each_sub(go)
        if base:
            pltpu.make_async_copy(src_base.at[me], dst.at[pl.ds(first(me), base)], own.at[stage, 0]).start()

    def back_extra(src_in, dst_in, src_extra, dst, stage, compute):
        if extra_any:
            @pl.when(has_extra(me))
            def _():
                spread_wait_extra(src_in, dst_in, stage - 1)
                src_extra[...] = compute()
                each_sub(lambda k, p: to_sub(src_extra.at[p], dst.at[first(me) + base], stage, 1, k, p).start())
                pltpu.make_async_copy(src_extra.at[me], dst.at[first(me) + base], own.at[stage, 1]).start()

    def back_wait(src_base, src_extra, dst, stage):
        if base:
            pltpu.make_async_copy(src_base.at[me], dst.at[pl.ds(first(me), base)], own.at[stage, 0]).wait()
        if extra_any:
            @pl.when(has_extra(me))
            def _():
                pltpu.make_async_copy(src_extra.at[me], dst.at[first(me) + base], own.at[stage, 1]).wait()

        def go(k, p):
            if base:
                from_sub(dst.at[pl.ds(first(p), base)], stage, 0, p)
            if extra_any:
                @pl.when(has_extra(p))
                def _():
                    from_sub(dst.at[first(p) + base], stage, 1, p)
        each_sub(go)

    def back_done(src_base, src_extra, dst, stage):
        if base:
            each_sub(lambda k, p: to_sub(src_base.at[p], dst.at[pl.ds(first(me), base)], stage, 0, k, p).wait_send())
        if extra_any:
            @pl.when(has_extra(me))
            def _():
                each_sub(lambda k, p: to_sub(src_extra.at[p], dst.at[first(me) + base], stage, 1, k, p).wait_send())

    def small_sub(src, dst, which, k, p):
        return pltpu.make_async_remote_copy(
            src_ref=src, dst_ref=dst.at[me], send_sem=small_send.at[which, k], recv_sem=small_recv.at[which, me],
            device_id={"sub": p}, device_id_type=pl.DeviceIdType.MESH)

    def small_sub_wait(dst, which, p):
        pltpu.make_async_remote_copy(
            src_ref=dst.at[p], dst_ref=dst.at[p], send_sem=small_send.at[which, 0], recv_sem=small_recv.at[which, p],
            device_id={"sub": p}, device_id_type=pl.DeviceIdType.MESH).wait_recv()

    def small_crs(src, dst, send_sem, recv_sem, k):
        return pltpu.make_async_remote_copy(
            src_ref=src, dst_ref=dst.at[mc], send_sem=send_sem.at[k], recv_sem=recv_sem.at[mc],
            device_id={"crs": lax.rem(mc + k, m)}, device_id_type=pl.DeviceIdType.MESH)

    def small_crs_wait(dst, send_sem, recv_sem, k):
        q = lax.rem(mc + k, m)
        pltpu.make_async_remote_copy(
            src_ref=dst.at[q], dst_ref=dst.at[q], send_sem=send_sem.at[0], recv_sem=recv_sem.at[q],
            device_id={"crs": q}, device_id_type=pl.DeviceIdType.MESH).wait_recv()

    pl.semaphore_wait(barrier, n - 1 + m - 1)
    spread(s1, rb1, rx1, 0)
    for c in small[2:]:
        c.wait()
    for k in range(1, m):
        small_crs(ci_ref, ci, ci_send, ci_recv, k).start()

    ci[mc] = ci_ref[...]
    assign_row = assign_ref[...]
    pick = iota((subs, subs), 0) == iota((subs, subs), 1)
    assign_col = jnp.sum(jnp.where(pick, assign_row, 0), axis=1, keepdims=True)
    slot_col = iota((rows_all, 1), 0) // rows_unit * slots + iota((rows_all, 1), 0) % slots
    a_col = jnp.sum(jnp.where(slot_col == iota((rows_all, subs), 1), assign_row, 0), axis=1, keepdims=True)
    slot_row = iota((1, rows_all), 1) // rows_unit * slots + iota((1, rows_all), 1) % slots
    a_row = jnp.sum(jnp.where(slot_row == iota((subs, rows_all), 0), assign_col, 0), axis=0, keepdims=True)
    side_col = iota((rows_all, 1), 0) // slots % 2
    side_row = iota((1, rows_all), 1) // slots % 2

    def plus(a, d):
        step = (4 * depth, depth, 1)[d]
        size = (4, 4, depth)[d]
        place = (a // step) % size
        return a + jnp.where(place == size - 1, step * (1 - size), step)

    for d in range(3):
        ahead = (plus(a_col, d) == a_row) & (side_col == 0) & (side_row == 1)
        behind = (a_col == plus(a_row, d)) & (side_col == 1) & (side_row == 0)
        perm[d] = jnp.where(ahead | behind, 1.0, 0.0).astype(BF16)

    lane = iota((1, LANES), 1)
    for p in range(patches):
        flags = solid_ref[:, p, :].astype(F32)
        for f in range(6):
            flag = flags[:, f:f + 1]
            at = row_of(0, f)
            for ct in range(tiles):
                low, high = p * entries - ct * LANES, (p + 1) * entries - ct * LANES
                if low >= LANES or high <= 0:
                    continue
                lanes = slice(ct * LANES, (ct + 1) * LANES)
                if low <= 0:
                    sm[at:at + slots, lanes] = jnp.broadcast_to(flag, (slots, LANES))
                else:
                    sm[at:at + slots, lanes] = jnp.where(lane >= low, flag, sm[at:at + slots, lanes])

    total = slots * nprim
    ncorner = nprim // 3
    part_col = iota((total, 1), 0)
    group = part_col // 3
    index = jnp.zeros((total, ncorner), jnp.int32)
    for l in range(slots):
        index = jnp.where(group == l * ncorner + iota((1, ncorner), 1), corners_ref[l:l + 1, :], index)
    index = 3 * jnp.sum(index, axis=1, keepdims=True) + part_col % 3
    hot = jnp.where(index == iota((total, coarse), 1), 1.0, 0.0).astype(F32)
    onehot[...] = hot
    onehot_t[...] = hot.T
    vt[...] = jnp.zeros_like(vt)
    col_row = iota((1, vt.shape[0]), 1) % rows_here
    sel[...] = jnp.zeros_like(sel)

    basis_load.wait()
    for f in range(6):
        faces_basis[f] = jnp.concatenate(
            [basis[l, f].astype(F32) for l in range(slots)], axis=0).astype(BF16)

    def restrict(u, j, r, k):
        p = perm[u // tiles]
        rh, rl = split2(r)
        kh, kl = split2(k)
        moved = jnp.dot(p, jnp.concatenate([rh, rl, kh, kl], axis=1), preferred_element_type=F32)
        rp = moved[:, :LANES] + moved[:, LANES:2 * LANES]
        kp = moved[:, 2 * LANES:3 * LANES] + moved[:, 3 * LANES:]
        scale = 1.0 / (k + kp)
        w = k * scale
        wts[j, 0] = w
        wts[j, 1] = kp * scale
        return (w * (r + rp)).reshape(n, rows_unit, LANES)

    spread_wait(s1, rb1, 0)
    for j in range(base):
        tb2[:, j] = restrict(
            first(me) + j, j, rb1[:, j, 0].reshape(rows_all, LANES), rb1[:, j, 1].reshape(rows_all, LANES))
    back(tb2, b2, 1)
    back_extra(s1, rx1, tx2, b2, 1, lambda: restrict(
        first(me) + base, base, rx1[:, 0].reshape(rows_all, LANES), rx1[:, 1].reshape(rows_all, LANES)))
    for k in range(1, m):
        small_crs_wait(ci, ci_send, ci_recv, k)
    ci_t[...] = ci[...].reshape(coarse, coarse).T
    back_wait(tb2, tx2, b2, 1)

    for d in range(3):
        for ct in range(tiles):
            lanes = slice(ct * LANES, (ct + 1) * LANES)
            group = slice(d * rows_unit, (d + 1) * rows_unit)
            value = sm[group, lanes] * b2[d * tiles + ct]
            for p in range(patches):
                low, high = p * entries - ct * LANES, (p + 1) * entries - ct * LANES
                if low >= LANES or high <= 0:
                    continue
                kept = value
                if low > 0:
                    kept = jnp.where(lane >= low, kept, 0.0)
                if high < LANES:
                    kept = jnp.where(lane < high, kept, 0.0)
                at = p * rows_here + d * rows_unit
                vt[at:at + rows_unit, lanes] = kept
    for ct in range(tiles):
        lanes = slice(ct * LANES, (ct + 1) * LANES)
        vectors_ref[lanes, :] = vt[:, lanes].T.astype(BF16)
    vectors = vectors_ref[...]
    columns = vectors.shape[1]

    products = jnp.dot(faces_basis[...].reshape(6 * total, width), vectors, preferred_element_type=F32)
    parts = []
    for l in range(slots):
        acc = jnp.zeros((nprim, columns), F32)
        for f in range(6):
            at = f * total + l * nprim
            acc = jnp.where(col_row == row_of(l, f), products[at:at + nprim], 0.0) + acc
        parts.append(acc)
    part = jnp.sum(jnp.concatenate(parts, axis=0), axis=1, keepdims=True)
    ca_s[...] = jnp.sum(part * onehot[...], axis=0, keepdims=True)
    ca_r[me] = ca_s[...]
    each_sub(lambda k, p: small_sub(ca_s, ca_r, 0, k, p).start())

    def solve(l):
        inv_load[l].wait()
        result = jnp.dot(inv[l].reshape(6 * entries, width), vectors, preferred_element_type=F32)
        total_sel = sel[0:entries, 0:columns]
        for f in range(6):
            total_sel = jnp.where(col_row == row_of(l, f), result[f * entries:(f + 1) * entries], total_sel)
        sel[0:entries, 0:columns] = total_sel

    half = (slots + 1) // 2
    for l in range(half):
        solve(l)
    each_sub(lambda k, p: small_sub_wait(ca_r, 0, p))
    cb_s[...] = jnp.sum(ca_r[...], axis=0)
    cb_r[mc] = cb_s[...]
    for k in range(1, m):
        small_crs(cb_s, cb_r, small_send.at[2], small_recv.at[2], k).start()
    for l in range(half, slots):
        solve(l)
    turned = sel[...].T
    for p in range(patches):
        loc[:, p * entries:(p + 1) * entries] = turned[p * rows_here:(p + 1) * rows_here, :entries]

    for k in range(1, m):
        small_crs_wait(cb_r, small_send.at[2], small_recv.at[2], k)
    residual_row = jnp.sum(cb_r[...], axis=0)
    coarse_solution = jnp.sum(ci_t[...] * residual_row, axis=1, keepdims=True)
    values = jnp.sum(onehot_t[...] * coarse_solution, axis=0, keepdims=True)
    slot_at = iota((rows_unit, 1), 0) % slots * nprim
    place = iota((1, total), 1)
    corner_values = jnp.where((place >= slot_at) & (place < slot_at + nprim), values, 0.0).astype(BF16)
    near = iota((rows_unit, 1), 0) < slots
    for d in range(3):
        corr[d * rows_unit:(d + 1) * rows_unit, :] = jnp.where(
            near,
            jnp.dot(corner_values, faces_basis[d], preferred_element_type=F32),
            jnp.dot(corner_values, faces_basis[d + 3], preferred_element_type=F32))

    inner = jnp.zeros((rows_unit, LANES), F32)
    for d in range(3):
        for ct in range(tiles):
            lanes = slice(ct * LANES, (ct + 1) * LANES)
            group = slice(d * rows_unit, (d + 1) * rows_unit)
            u = sm[group, lanes] * (loc[group, lanes] + corr[group, lanes])
            s3[d * tiles + ct] = u
            inner = inner + u * b2[d * tiles + ct]
    spread(s3, rb3, rx3, 2)
    ia_s[...] = jnp.sum(inner, axis=0, keepdims=True)
    ia_r[me] = ia_s[...]
    each_sub(lambda k, p: small_sub(ia_s, ia_r, 1, k, p).start())

    def average(u, j, x):
        xh, xl = split2(x)
        moved = jnp.dot(perm[u // tiles], jnp.concatenate([xh, xl], axis=1), preferred_element_type=F32)
        xp = moved[:, :LANES] + moved[:, LANES:]
        return (wts[j, 0] * x + wts[j, 1] * xp).reshape(n, rows_unit, LANES)

    spread_wait(s3, rb3, 2)
    for j in range(base):
        tb4[:, j] = average(first(me) + j, j, rb3[:, j].reshape(rows_all, LANES))
    back(tb4, b4, 3)
    back_extra(s3, rx3, tx4, b4, 3, lambda: average(first(me) + base, base, rx3[...].reshape(rows_all, LANES)))
    each_sub(lambda k, p: small_sub_wait(ia_r, 1, p))
    ib_s[...] = jnp.sum(ia_r[...], axis=0)
    ib_r[mc] = ib_s[...]
    for k in range(1, m):
        small_crs(ib_s, ib_r, small_send.at[3], small_recv.at[3], k).start()

    spread_done(s1, rb1, rx1, 0)
    back_done(tb2, tx2, b2, 1)
    spread_done(s3, rb3, rx3, 2)
    for k in range(1, m):
        small_crs(ci_ref, ci, ci_send, ci_recv, k).wait_send()
        small_crs(cb_s, cb_r, small_send.at[2], small_recv.at[2], k).wait_send()
    each_sub(lambda k, p: small_sub(ca_s, ca_r, 0, k, p).wait_send())
    each_sub(lambda k, p: small_sub(ia_s, ia_r, 1, k, p).wait_send())

    back_wait(tb4, tx4, b4, 3)
    for f in range(6):
        for ct in range(tiles):
            row = (f // 3) * slots
            out_ref[f, :, ct * LANES:(ct + 1) * LANES] = b4[(f % 3) * tiles + ct, row:row + slots, :]
    for k in range(1, m):
        small_crs_wait(ib_r, small_send.at[3], small_recv.at[3], k)
    inner_ref[...] = jnp.sum(jnp.sum(ib_r[...], axis=0), axis=1, keepdims=True)
    back_done(tb4, tx4, b4, 3)
    for k in range(1, m):
        small_crs(ib_s, ib_r, small_send.at[3], small_recv.at[3], k).wait_send()


def body(residual, stiffness, solid, inverses, coarse_basis, assign, corners, coarse_inverse):
    slots, faces, width = residual.shape
    patches = solid.shape[2]
    entries = width // patches
    n, m = lax.axis_size("sub"), lax.axis_size("crs")
    subs = assign.shape[0]
    tiles = width // LANES
    units = 3 * tiles
    base = units // n
    rows = 2 * slots
    rows_all = n * rows
    nprim = coarse_basis.shape[1]
    coarse = coarse_inverse.shape[1]
    cfg = (n, m, slots, tiles, patches, entries, subs)
    kept = max(base, 1)
    vt_rows = -(-(patches * rows * 3) // LANES) * LANES
    square = -(-entries // LANES) * LANES
    vmem = pl.BlockSpec(memory_space=pltpu.VMEM)
    anyw = pl.BlockSpec(memory_space=pl.ANY)
    size = max(n, m)
    out, inner = pl.pallas_call(
        functools.partial(kernel, cfg),
        out_shape=(
            jax.ShapeDtypeStruct((faces, slots, width), F32),
            jax.ShapeDtypeStruct((1, 1), F32),
        ),
        in_specs=[anyw] * 8,
        out_specs=(vmem, vmem),
        scratch_shapes=[
            pltpu.VMEM((faces, slots, width), F32),
            pltpu.VMEM((faces, slots, width), F32),
            pltpu.VMEM((slots, patches, faces), jnp.int32),
            pltpu.VMEM((1, subs), jnp.int32),
            pltpu.VMEM(corners.shape, jnp.int32),
            pltpu.VMEM(coarse_inverse.shape, F32),
            pltpu.VMEM(inverses.shape, BF16),
            pltpu.VMEM((slots, faces, nprim, width), BF16),
            pltpu.VMEM((faces, slots * nprim, width), BF16),
            pltpu.VMEM((units, 2, rows, LANES), F32),
            pltpu.VMEM((n, kept, 2, rows, LANES), F32),
            pltpu.VMEM((n, 2, rows, LANES), F32),
            pltpu.VMEM((base + 1, 2, rows_all, LANES), F32),
            pltpu.VMEM((n, kept, rows, LANES), F32),
            pltpu.VMEM((n, rows, LANES), F32),
            pltpu.VMEM((units, rows, LANES), F32),
            pltpu.VMEM((units, rows, LANES), F32),
            pltpu.VMEM((n, kept, rows, LANES), F32),
            pltpu.VMEM((n, rows, LANES), F32),
            pltpu.VMEM((n, kept, rows, LANES), F32),
            pltpu.VMEM((n, rows, LANES), F32),
            pltpu.VMEM((units, rows, LANES), F32),
            pltpu.VMEM((3, rows_all, rows_all), BF16),
            pltpu.VMEM((3 * rows, width), F32),
            pltpu.VMEM((3 * rows, width), F32),
            pltpu.VMEM((3 * rows, width), F32),
            pltpu.VMEM((vt_rows, width), F32),
            pltpu.VMEM((width, vt_rows), BF16),
            pltpu.VMEM((square, vt_rows), F32),
            pltpu.VMEM((slots * nprim, coarse), F32),
            pltpu.VMEM((coarse, slots * nprim), F32),
            pltpu.VMEM((m,) + coarse_inverse.shape, F32),
            pltpu.VMEM((coarse, coarse), F32),
            pltpu.VMEM((1, coarse), F32),
            pltpu.VMEM((n, 1, coarse), F32),
            pltpu.VMEM((1, coarse), F32),
            pltpu.VMEM((m, 1, coarse), F32),
            pltpu.VMEM((1, LANES), F32),
            pltpu.VMEM((n, 1, LANES), F32),
            pltpu.VMEM((1, LANES), F32),
            pltpu.VMEM((m, 1, LANES), F32),
            pltpu.SemaphoreType.DMA((4, 2, n)),
            pltpu.SemaphoreType.DMA((4, 2, n)),
            pltpu.SemaphoreType.DMA((4, 2)),
            pltpu.SemaphoreType.DMA((slots + 1,)),
            pltpu.SemaphoreType.DMA((6,)),
            pltpu.SemaphoreType.DMA((4, size)),
            pltpu.SemaphoreType.DMA((4, size)),
            pltpu.SemaphoreType.DMA((m,)),
            pltpu.SemaphoreType.DMA((m,)),
        ],
        compiler_params=pltpu.CompilerParams(
            collective_id=0, has_side_effects=True, vmem_limit_bytes=60 * 1024 * 1024
        ),
    )(
        residual.transpose(1, 0, 2), stiffness.transpose(1, 0, 2), solid.transpose(0, 2, 1), inverses,
        coarse_basis.transpose(0, 2, 1, 3), assign.reshape(1, subs), corners, coarse_inverse)
    return out.transpose(1, 0, 2), inner.reshape(1)


def solution(mesh):
    return jax.shard_map(
        body,
        mesh=mesh,
        in_specs=(
            P("sub", None, "crs"),
            P("sub", None, "crs"),
            P("sub", None, "crs"),
            P("sub", None, None, "crs"),
            P("sub", None, None, "crs"),
            P(),
            P("sub", None),
            P("crs", None),
        ),
        out_specs=(P("sub", None, "crs"), P()),
        check_vma=False,
    )
```

```python
import functools

import jax
import jax.numpy as jnp
from jax import lax
from jax.experimental import pallas as pl
from jax.experimental.pallas import tpu as pltpu
from jax.sharding import PartitionSpec as P

F32 = jnp.float32
BF16 = jnp.bfloat16
LANES = 128


def iota(shape, dim):
    return lax.broadcasted_iota(jnp.int32, shape, dim)


def split2(x):
    high = x.astype(BF16)
    low = (x - high.astype(F32)).astype(BF16)
    return high, low


def kernel(
    cfg,
    r_hbm, k_hbm, solid_hbm, inv_hbm, basis_hbm, assign_hbm, corners_hbm, ci_hbm,
    out_ref, inner_ref,
    r_ref, k_ref, solid_ref, assign_ref, corners_ref, ci_ref,
    inv, basis, faces_basis, s1, rb1, rx1, wts, tb2, tx2, b2, s3, rb3, rx3, tb4, tx4, b4,
    perm, sm, loc, corr, vt, vectors_ref, sel, onehot, onehot_t, ci, ci_t,
    ca_s, ca_r, cb_s, cb_r, ia_s, ia_r, ib_s, ib_r,
    send, recv, own, load, small_load, small_send, small_recv, ci_send, ci_recv,
):
    n, m, slots, tiles, patches, entries, subs = cfg
    depth = subs // 16
    units = 3 * tiles
    base = units // n
    extra_any = units % n != 0
    rows_unit = 2 * slots
    rows_all = n * rows_unit
    rows_here = 6 * slots
    width = tiles * LANES
    nprim = basis.shape[2]
    coarse = ci_ref.shape[1]
    me = lax.axis_index("sub")
    mc = lax.axis_index("crs")

    def first(p):
        return (p * units + n - 1) // n

    def has_extra(p):
        return first(p + 1) - first(p) > base

    def row_of(l, f):
        return (f % 3) * rows_unit + (f // 3) * slots + l

    small = [
        pltpu.make_async_copy(src, dst, small_load.at[i])
        for i, (src, dst) in enumerate((
            (r_hbm, r_ref), (k_hbm, k_ref), (ci_hbm, ci_ref), (assign_hbm, assign_ref),
            (solid_hbm, solid_ref), (corners_hbm, corners_ref)))
    ]
    for c in small:
        c.start()
    basis_load = pltpu.make_async_copy(basis_hbm, basis, load.at[slots])
    basis_load.start()
    inv_load = [pltpu.make_async_copy(inv_hbm.at[l], inv.at[l], load.at[l]) for l in range(slots)]
    for c in inv_load:
        c.start()

    def each_sub(body):
        if n <= 8:
            for k in range(1, n):
                body(k, lax.rem(me + k, n))
        else:
            def step(k, carry):
                body(k, lax.rem(me + k, n))
                return carry
            lax.fori_loop(1, n, step, 0)

    barrier = pltpu.get_barrier_semaphore()

    def greet(k, p):
        pl.semaphore_signal(barrier, inc=1, device_id={"sub": p}, device_id_type=pl.DeviceIdType.MESH)

    each_sub(greet)
    for k in range(1, m):
        pl.semaphore_signal(barrier, inc=1, device_id={"crs": lax.rem(mc + k, m)}, device_id_type=pl.DeviceIdType.MESH)

    for a, ref in enumerate((r_ref, k_ref)):
        small[a].wait()
        for f in range(6):
            for ct in range(tiles):
                row = (f // 3) * slots
                s1[(f % 3) * tiles + ct, a, row:row + slots, :] = ref[f, :, ct * LANES:(ct + 1) * LANES]

    def to_sub(src, dst, stage, kind, k, p):
        return pltpu.make_async_remote_copy(
            src_ref=src, dst_ref=dst, send_sem=send.at[stage, kind, k], recv_sem=recv.at[stage, kind, me],
            device_id={"sub": p}, device_id_type=pl.DeviceIdType.MESH)

    def from_sub(dst, stage, kind, p):
        pltpu.make_async_remote_copy(
            src_ref=dst, dst_ref=dst, send_sem=send.at[stage, kind, 0], recv_sem=recv.at[stage, kind, p],
            device_id={"sub": p}, device_id_type=pl.DeviceIdType.MESH).wait_recv()

    def spread(src, dst_base, dst_extra, stage):
        def go(k, p):
            if base:
                to_sub(src.at[pl.ds(first(p), base)], dst_base.at[me], stage, 0, k, p).start()
            if extra_any:
                @pl.when(has_extra(p))
                def _():
                    to_sub(src.at[first(p) + base], dst_extra.at[me], stage, 1, k, p).start()
        each_sub(go)
        if base:
            pltpu.make_async_copy(src.at[pl.ds(first(me), base)], dst_base.at[me], own.at[stage, 0]).start()
        if extra_any:
            @pl.when(has_extra(me))
            def _():
                pltpu.make_async_copy(src.at[first(me) + base], dst_extra.at[me], own.at[stage, 1]).start()

    def spread_wait(src, dst_base, stage):
        if base:
            pltpu.make_async_copy(src.at[pl.ds(first(me), base)], dst_base.at[me], own.at[stage, 0]).wait()
            each_sub(lambda k, p: from_sub(dst_base.at[p], stage, 0, p))

    def spread_wait_extra(src, dst_extra, stage):
        pltpu.make_async_copy(src.at[first(me) + base], dst_extra.at[me], own.at[stage, 1]).wait()
        each_sub(lambda k, p: from_sub(dst_extra.at[p], stage, 1, p))

    def spread_done(src, dst_base, dst_extra, stage):
        def go(k, p):
            if base:
                to_sub(src.at[pl.ds(first(p), base)], dst_base.at[me], stage, 0, k, p).wait_send()
            if extra_any:
                @pl.when(has_extra(p))
                def _():
                    to_sub(src.at[first(p) + base], dst_extra.at[me], stage, 1, k, p).wait_send()
        each_sub(go)

    def back(src_base, dst, stage):
        def go(k, p):
            if base:
                to_sub(src_base.at[p], dst.at[pl.ds(first(me), base)], stage, 0, k, p).start()
        each_sub(go)
        if base:
            pltpu.make_async_copy(src_base.at[me], dst.at[pl.ds(first(me), base)], own.at[stage, 0]).start()

    def back_extra(src_in, dst_in, src_extra, dst, stage, compute):
        if extra_any:
            @pl.when(has_extra(me))
            def _():
                spread_wait_extra(src_in, dst_in, stage - 1)
                src_extra[...] = compute()
                each_sub(lambda k, p: to_sub(src_extra.at[p], dst.at[first(me) + base], stage, 1, k, p).start())
                pltpu.make_async_copy(src_extra.at[me], dst.at[first(me) + base], own.at[stage, 1]).start()

    def back_wait(src_base, src_extra, dst, stage):
        if base:
            pltpu.make_async_copy(src_base.at[me], dst.at[pl.ds(first(me), base)], own.at[stage, 0]).wait()
        if extra_any:
            @pl.when(has_extra(me))
            def _():
                pltpu.make_async_copy(src_extra.at[me], dst.at[first(me) + base], own.at[stage, 1]).wait()

        def go(k, p):
            if base:
                from_sub(dst.at[pl.ds(first(p), base)], stage, 0, p)
            if extra_any:
                @pl.when(has_extra(p))
                def _():
                    from_sub(dst.at[first(p) + base], stage, 1, p)
        each_sub(go)

    def back_done(src_base, src_extra, dst, stage):
        if base:
            each_sub(lambda k, p: to_sub(src_base.at[p], dst.at[pl.ds(first(me), base)], stage, 0, k, p).wait_send())
        if extra_any:
            @pl.when(has_extra(me))
            def _():
                each_sub(lambda k, p: to_sub(src_extra.at[p], dst.at[first(me) + base], stage, 1, k, p).wait_send())

    def small_sub(src, dst, which, k, p):
        return pltpu.make_async_remote_copy(
            src_ref=src, dst_ref=dst.at[me], send_sem=small_send.at[which, k], recv_sem=small_recv.at[which, me],
            device_id={"sub": p}, device_id_type=pl.DeviceIdType.MESH)

    def small_sub_wait(dst, which, p):
        pltpu.make_async_remote_copy(
            src_ref=dst.at[p], dst_ref=dst.at[p], send_sem=small_send.at[which, 0], recv_sem=small_recv.at[which, p],
            device_id={"sub": p}, device_id_type=pl.DeviceIdType.MESH).wait_recv()

    def small_crs(src, dst, send_sem, recv_sem, k):
        return pltpu.make_async_remote_copy(
            src_ref=src, dst_ref=dst.at[mc], send_sem=send_sem.at[k], recv_sem=recv_sem.at[mc],
            device_id={"crs": lax.rem(mc + k, m)}, device_id_type=pl.DeviceIdType.MESH)

    def small_crs_wait(dst, send_sem, recv_sem, k):
        q = lax.rem(mc + k, m)
        pltpu.make_async_remote_copy(
            src_ref=dst.at[q], dst_ref=dst.at[q], send_sem=send_sem.at[0], recv_sem=recv_sem.at[q],
            device_id={"crs": q}, device_id_type=pl.DeviceIdType.MESH).wait_recv()

    pl.semaphore_wait(barrier, n - 1 + m - 1)
    spread(s1, rb1, rx1, 0)
    for c in small[2:]:
        c.wait()
    for k in range(1, m):
        small_crs(ci_ref, ci, ci_send, ci_recv, k).start()

    ci[mc] = ci_ref[...]
    assign_row = assign_ref[...]
    pick = iota((subs, subs), 0) == iota((subs, subs), 1)
    assign_col = jnp.sum(jnp.where(pick, assign_row, 0), axis=1, keepdims=True)
    slot_col = iota((rows_all, 1), 0) // rows_unit * slots + iota((rows_all, 1), 0) % slots
    a_col = jnp.sum(jnp.where(slot_col == iota((rows_all, subs), 1), assign_row, 0), axis=1, keepdims=True)
    slot_row = iota((1, rows_all), 1) // rows_unit * slots + iota((1, rows_all), 1) % slots
    a_row = jnp.sum(jnp.where(slot_row == iota((subs, rows_all), 0), assign_col, 0), axis=0, keepdims=True)
    side_col = iota((rows_all, 1), 0) // slots % 2
    side_row = iota((1, rows_all), 1) // slots % 2

    def plus(a, d):
        step = (4 * depth, depth, 1)[d]
        size = (4, 4, depth)[d]
        place = (a // step) % size
        return a + jnp.where(place == size - 1, step * (1 - size), step)

    for d in range(3):
        ahead = (plus(a_col, d) == a_row) & (side_col == 0) & (side_row == 1)
        behind = (a_col == plus(a_row, d)) & (side_col == 1) & (side_row == 0)
        perm[d] = jnp.where(ahead | behind, 1.0, 0.0).astype(BF16)

    lane = iota((1, LANES), 1)
    for p in range(patches):
        flags = solid_ref[:, p, :].astype(F32)
        for f in range(6):
            flag = flags[:, f:f + 1]
            at = row_of(0, f)
            for ct in range(tiles):
                low, high = p * entries - ct * LANES, (p + 1) * entries - ct * LANES
                if low >= LANES or high <= 0:
                    continue
                lanes = slice(ct * LANES, (ct + 1) * LANES)
                if low <= 0:
                    sm[at:at + slots, lanes] = jnp.broadcast_to(flag, (slots, LANES))
                else:
                    sm[at:at + slots, lanes] = jnp.where(lane >= low, flag, sm[at:at + slots, lanes])

    def restrict(u, j, r, k):
        p = perm[u // tiles]
        rh, rl = split2(r)
        kh, kl = split2(k)
        moved = jnp.dot(p, jnp.concatenate([rh, rl, kh, kl], axis=1), preferred_element_type=F32)
        rp = moved[:, :LANES] + moved[:, LANES:2 * LANES]
        kp = moved[:, 2 * LANES:3 * LANES] + moved[:, 3 * LANES:]
        scale = 1.0 / (k + kp)
        w = k * scale
        wts[j, 0] = w
        wts[j, 1] = kp * scale
        return (w * (r + rp)).reshape(n, rows_unit, LANES)

    spread_wait(s1, rb1, 0)
    for j in range(base):
        tb2[:, j] = restrict(
            first(me) + j, j, rb1[:, j, 0].reshape(rows_all, LANES), rb1[:, j, 1].reshape(rows_all, LANES))
    back(tb2, b2, 1)
    back_extra(s1, rx1, tx2, b2, 1, lambda: restrict(
        first(me) + base, base, rx1[:, 0].reshape(rows_all, LANES), rx1[:, 1].reshape(rows_all, LANES)))
    total = slots * nprim
    ncorner = nprim // 3
    part_col = iota((total, 1), 0)
    group = part_col // 3
    index = jnp.zeros((total, ncorner), jnp.int32)
    for l in range(slots):
        index = jnp.where(group == l * ncorner + iota((1, ncorner), 1), corners_ref[l:l + 1, :], index)
    index = 3 * jnp.sum(index, axis=1, keepdims=True) + part_col % 3
    hot = jnp.where(index == iota((total, coarse), 1), 1.0, 0.0).astype(F32)
    onehot[...] = hot
    onehot_t[...] = hot.T
    vt[...] = jnp.zeros_like(vt)
    col_row = iota((1, vt.shape[0]), 1) % rows_here
    sel[...] = jnp.zeros_like(sel)

    basis_load.wait()
    for f in range(6):
        faces_basis[f] = jnp.concatenate(
            [basis[l, f].astype(F32) for l in range(slots)], axis=0).astype(BF16)

    for k in range(1, m):
        small_crs_wait(ci, ci_send, ci_recv, k)
    ci_t[...] = ci[...].reshape(coarse, coarse).T
    back_wait(tb2, tx2, b2, 1)

    for d in range(3):
        for ct in range(tiles):
            lanes = slice(ct * LANES, (ct + 1) * LANES)
            group = slice(d * rows_unit, (d + 1) * rows_unit)
            value = sm[group, lanes] * b2[d * tiles + ct]
            for p in range(patches):
                low, high = p * entries - ct * LANES, (p + 1) * entries - ct * LANES
                if low >= LANES or high <= 0:
                    continue
                kept = value
                if low > 0:
                    kept = jnp.where(lane >= low, kept, 0.0)
                if high < LANES:
                    kept = jnp.where(lane < high, kept, 0.0)
                at = p * rows_here + d * rows_unit
                vt[at:at + rows_unit, lanes] = kept
    for ct in range(tiles):
        lanes = slice(ct * LANES, (ct + 1) * LANES)
        vectors_ref[lanes, :] = vt[:, lanes].T.astype(BF16)
    vectors = vectors_ref[...]
    columns = vectors.shape[1]

    products = jnp.dot(faces_basis[...].reshape(6 * total, width), vectors, preferred_element_type=F32)
    parts = []
    for l in range(slots):
        acc = jnp.zeros((nprim, columns), F32)
        for f in range(6):
            at = f * total + l * nprim
            acc = jnp.where(col_row == row_of(l, f), products[at:at + nprim], 0.0) + acc
        parts.append(acc)
    part = jnp.sum(jnp.concatenate(parts, axis=0), axis=1, keepdims=True)
    ca_s[...] = jnp.sum(part * onehot[...], axis=0, keepdims=True)
    ca_r[me] = ca_s[...]
    each_sub(lambda k, p: small_sub(ca_s, ca_r, 0, k, p).start())

    def solve(l):
        inv_load[l].wait()
        result = jnp.dot(inv[l].reshape(6 * entries, width), vectors, preferred_element_type=F32)
        total_sel = sel[0:entries, 0:columns]
        for f in range(6):
            total_sel = jnp.where(col_row == row_of(l, f), result[f * entries:(f + 1) * entries], total_sel)
        sel[0:entries, 0:columns] = total_sel

    half = (slots + 1) // 2
    for l in range(half):
        solve(l)
    each_sub(lambda k, p: small_sub_wait(ca_r, 0, p))
    cb_s[...] = jnp.sum(ca_r[...], axis=0)
    cb_r[mc] = cb_s[...]
    for k in range(1, m):
        small_crs(cb_s, cb_r, small_send.at[2], small_recv.at[2], k).start()
    for l in range(half, slots):
        solve(l)
    turned = sel[...].T
    for p in range(patches):
        loc[:, p * entries:(p + 1) * entries] = turned[p * rows_here:(p + 1) * rows_here, :entries]

    for k in range(1, m):
        small_crs_wait(cb_r, small_send.at[2], small_recv.at[2], k)
    residual_row = jnp.sum(cb_r[...], axis=0)
    coarse_solution = jnp.sum(ci_t[...] * residual_row, axis=1, keepdims=True)
    values = jnp.sum(onehot_t[...] * coarse_solution, axis=0, keepdims=True)
    slot_at = iota((rows_unit, 1), 0) % slots * nprim
    place = iota((1, total), 1)
    corner_values = jnp.where((place >= slot_at) & (place < slot_at + nprim), values, 0.0).astype(BF16)
    near = iota((rows_unit, 1), 0) < slots
    for d in range(3):
        corr[d * rows_unit:(d + 1) * rows_unit, :] = jnp.where(
            near,
            jnp.dot(corner_values, faces_basis[d], preferred_element_type=F32),
            jnp.dot(corner_values, faces_basis[d + 3], preferred_element_type=F32))

    inner = jnp.zeros((rows_unit, LANES), F32)
    for d in range(3):
        for ct in range(tiles):
            lanes = slice(ct * LANES, (ct + 1) * LANES)
            group = slice(d * rows_unit, (d + 1) * rows_unit)
            u = sm[group, lanes] * (loc[group, lanes] + corr[group, lanes])
            s3[d * tiles + ct] = u
            inner = inner + u * b2[d * tiles + ct]
    spread(s3, rb3, rx3, 2)
    ia_s[...] = jnp.sum(inner, axis=0, keepdims=True)
    ia_r[me] = ia_s[...]
    each_sub(lambda k, p: small_sub(ia_s, ia_r, 1, k, p).start())

    def average(u, j, x):
        xh, xl = split2(x)
        moved = jnp.dot(perm[u // tiles], jnp.concatenate([xh, xl], axis=1), preferred_element_type=F32)
        xp = moved[:, :LANES] + moved[:, LANES:]
        return (wts[j, 0] * x + wts[j, 1] * xp).reshape(n, rows_unit, LANES)

    spread_wait(s3, rb3, 2)
    for j in range(base):
        tb4[:, j] = average(first(me) + j, j, rb3[:, j].reshape(rows_all, LANES))
    back(tb4, b4, 3)
    back_extra(s3, rx3, tx4, b4, 3, lambda: average(first(me) + base, base, rx3[...].reshape(rows_all, LANES)))
    each_sub(lambda k, p: small_sub_wait(ia_r, 1, p))
    ib_s[...] = jnp.sum(ia_r[...], axis=0)
    ib_r[mc] = ib_s[...]
    for k in range(1, m):
        small_crs(ib_s, ib_r, small_send.at[3], small_recv.at[3], k).start()

    spread_done(s1, rb1, rx1, 0)
    back_done(tb2, tx2, b2, 1)
    spread_done(s3, rb3, rx3, 2)
    for k in range(1, m):
        small_crs(ci_ref, ci, ci_send, ci_recv, k).wait_send()
        small_crs(cb_s, cb_r, small_send.at[2], small_recv.at[2], k).wait_send()
    each_sub(lambda k, p: small_sub(ca_s, ca_r, 0, k, p).wait_send())
    each_sub(lambda k, p: small_sub(ia_s, ia_r, 1, k, p).wait_send())

    back_wait(tb4, tx4, b4, 3)
    for f in range(6):
        for ct in range(tiles):
            row = (f // 3) * slots
            out_ref[f, :, ct * LANES:(ct + 1) * LANES] = b4[(f % 3) * tiles + ct, row:row + slots, :]
    for k in range(1, m):
        small_crs_wait(ib_r, small_send.at[3], small_recv.at[3], k)
    inner_ref[...] = jnp.sum(jnp.sum(ib_r[...], axis=0), axis=1, keepdims=True)
    back_done(tb4, tx4, b4, 3)
    for k in range(1, m):
        small_crs(ib_s, ib_r, small_send.at[3], small_recv.at[3], k).wait_send()


def body(residual, stiffness, solid, inverses, coarse_basis, assign, corners, coarse_inverse):
    slots, faces, width = residual.shape
    patches = solid.shape[2]
    entries = width // patches
    n, m = lax.axis_size("sub"), lax.axis_size("crs")
    subs = assign.shape[0]
    tiles = width // LANES
    units = 3 * tiles
    base = units // n
    rows = 2 * slots
    rows_all = n * rows
    nprim = coarse_basis.shape[1]
    coarse = coarse_inverse.shape[1]
    cfg = (n, m, slots, tiles, patches, entries, subs)
    kept = max(base, 1)
    vt_rows = -(-(patches * rows * 3) // LANES) * LANES
    square = -(-entries // LANES) * LANES
    vmem = pl.BlockSpec(memory_space=pltpu.VMEM)
    anyw = pl.BlockSpec(memory_space=pl.ANY)
    size = max(n, m)
    out, inner = pl.pallas_call(
        functools.partial(kernel, cfg),
        out_shape=(
            jax.ShapeDtypeStruct((faces, slots, width), F32),
            jax.ShapeDtypeStruct((1, 1), F32),
        ),
        in_specs=[anyw] * 8,
        out_specs=(vmem, vmem),
        scratch_shapes=[
            pltpu.VMEM((faces, slots, width), F32),
            pltpu.VMEM((faces, slots, width), F32),
            pltpu.VMEM((slots, patches, faces), jnp.int32),
            pltpu.VMEM((1, subs), jnp.int32),
            pltpu.VMEM(corners.shape, jnp.int32),
            pltpu.VMEM(coarse_inverse.shape, F32),
            pltpu.VMEM(inverses.shape, BF16),
            pltpu.VMEM((slots, faces, nprim, width), BF16),
            pltpu.VMEM((faces, slots * nprim, width), BF16),
            pltpu.VMEM((units, 2, rows, LANES), F32),
            pltpu.VMEM((n, kept, 2, rows, LANES), F32),
            pltpu.VMEM((n, 2, rows, LANES), F32),
            pltpu.VMEM((base + 1, 2, rows_all, LANES), F32),
            pltpu.VMEM((n, kept, rows, LANES), F32),
            pltpu.VMEM((n, rows, LANES), F32),
            pltpu.VMEM((units, rows, LANES), F32),
            pltpu.VMEM((units, rows, LANES), F32),
            pltpu.VMEM((n, kept, rows, LANES), F32),
            pltpu.VMEM((n, rows, LANES), F32),
            pltpu.VMEM((n, kept, rows, LANES), F32),
            pltpu.VMEM((n, rows, LANES), F32),
            pltpu.VMEM((units, rows, LANES), F32),
            pltpu.VMEM((3, rows_all, rows_all), BF16),
            pltpu.VMEM((3 * rows, width), F32),
            pltpu.VMEM((3 * rows, width), F32),
            pltpu.VMEM((3 * rows, width), F32),
            pltpu.VMEM((vt_rows, width), F32),
            pltpu.VMEM((width, vt_rows), BF16),
            pltpu.VMEM((square, vt_rows), F32),
            pltpu.VMEM((slots * nprim, coarse), F32),
            pltpu.VMEM((coarse, slots * nprim), F32),
            pltpu.VMEM((m,) + coarse_inverse.shape, F32),
            pltpu.VMEM((coarse, coarse), F32),
            pltpu.VMEM((1, coarse), F32),
            pltpu.VMEM((n, 1, coarse), F32),
            pltpu.VMEM((1, coarse), F32),
            pltpu.VMEM((m, 1, coarse), F32),
            pltpu.VMEM((1, LANES), F32),
            pltpu.VMEM((n, 1, LANES), F32),
            pltpu.VMEM((1, LANES), F32),
            pltpu.VMEM((m, 1, LANES), F32),
            pltpu.SemaphoreType.DMA((4, 2, n)),
            pltpu.SemaphoreType.DMA((4, 2, n)),
            pltpu.SemaphoreType.DMA((4, 2)),
            pltpu.SemaphoreType.DMA((slots + 1,)),
            pltpu.SemaphoreType.DMA((6,)),
            pltpu.SemaphoreType.DMA((4, size)),
            pltpu.SemaphoreType.DMA((4, size)),
            pltpu.SemaphoreType.DMA((m,)),
            pltpu.SemaphoreType.DMA((m,)),
        ],
        compiler_params=pltpu.CompilerParams(
            collective_id=0, has_side_effects=True, vmem_limit_bytes=60 * 1024 * 1024
        ),
    )(
        residual.transpose(1, 0, 2), stiffness.transpose(1, 0, 2), solid.transpose(0, 2, 1), inverses,
        coarse_basis.transpose(0, 2, 1, 3), assign.reshape(1, subs), corners, coarse_inverse)
    return out.transpose(1, 0, 2), inner.reshape(1)


def solution(mesh):
    return jax.shard_map(
        body,
        mesh=mesh,
        in_specs=(
            P("sub", None, "crs"),
            P("sub", None, "crs"),
            P("sub", None, "crs"),
            P("sub", None, None, "crs"),
            P("sub", None, None, "crs"),
            P(),
            P("sub", None),
            P("crs", None),
        ),
        out_specs=(P("sub", None, "crs"), P()),
        check_vma=False,
    )
```
